32 devices in a mesh: wide: 32 (over z, y, x, core), batch: 1.
Axes of the slice: x: 2, y: 2, z: 4, core: 2. Of those that a mesh axis runs over, the one named last changes fastest.
Arguments:
- q_latent: bfloat16 [1, 64, 4, 1536], P('batch', 'wide'), may hold values from -6 to 6
- draft_start: int32 [1, 64], P('batch', 'wide'), may hold values from 4096 to 8191
- cache_len: int32 [1, 64], P('batch', 'wide'), may hold values from 1 to 4092, 163680 in all within a row
- latent_cache: bfloat16 [1, 64, 4096, 576], P('batch', 'wide'), may hold values from -576 to 576
- w_q_up: bfloat16 [1536, 24576], P('batch', 'wide'), may hold values from -0.15625 to 0.15625
- w_k_absorb: bfloat16 [128, 128, 512], P('wide'), may hold values from -0.5 to 0.5
- value_up_weight: bfloat16 [128, 512, 128], P('wide'), may hold values from -0.25 to 0.25
Outputs:
- values: bfloat16 [1, 64, 4, 16384], P('batch', None, None, 'wide')
The draws below stay inside these ranges and needn't reach their ends.
All inputs are finite; a program needn't handle non-finite values. No bound on the sum of `cache_len` on one device may be relied on, other than what follows from the above.
Results may differ from the reference program's by a relative error of at most 0.014.
The reference program's roundings to bfloat16 on the way count: a program that leaves them out, or rounds other values in their place, can miss the bound.
Values may be sent and summed in bfloat16 or wider, within the bound.
A program may use at most 128 MiB of HBM per device.

```python
import math
import jax
import jax.numpy as jnp
import numpy as np
from jax import lax

QL = 1536
HEADS = 128
NOPE = 128
ROPE = 64
KVL = 512
VD = 128
DRAFT = 4
CTX = 4096
REQUESTS_GROUP = 64
GROUPS = 1


def draw_latent_cache(key, part):
    base = 1.5 * jax.random.truncated_normal(key, -6.0, 6.0, (GROUPS, REQUESTS_GROUP, CTX, KVL + ROPE), jnp.float32)
    return base.astype(jnp.bfloat16)


def plant(entries, rng, smallest, high):
    index_at = [jax.random.randint(jax.random.fold_in(rng, axis), (), 0, length) for axis, length in enumerate(entries.shape)]
    longest = entries.shape.index(max(entries.shape))
    beside = index_at[:longest] + [(index_at[longest] + 1) % entries.shape[longest]] + index_at[longest + 1:]
    return entries.at[tuple(index_at)].set(smallest).at[tuple(beside)].set(high)


def steps_of(stream_key, shape, shards, smallest, high):
    level, own = 1.0, jax.random.fold_in(stream_key, 6)
    for position, shards_of in shards:
        draws = jnp.exp(jax.random.uniform(jax.random.fold_in(own, position), (shards_of,), jnp.float32, smallest / len(shards), high / len(shards)))
        level = level * jnp.repeat(draws, shape[position] // shards_of).reshape([-1 if axis == position else 1 for axis in range(len(shape))])
    return level


def profile(number_of, total, bound, skew):
    loads = [(1 << 20) // math.isqrt(rank ** skew) + 1 for rank in range(2, number_of + 1)]
    surplus, holding = total - bound - (number_of - 1), [1] * (number_of - 1)
    while surplus > 0:
        free = [i for i in range(number_of - 1) if holding[i] < bound]
        pool, budget = sum([loads[i] for i in free]), surplus
        for i in free:
            more = min(bound - holding[i], max(1, budget * loads[i] // pool), surplus)
            holding[i] = holding[i] + more
            surplus = surplus - more
    return np.array([bound] + holding)


def ragged_sizes(stream_key, number_of, total, most, slope):
    if number_of == 2:
        one = jax.random.randint(stream_key, (), max(1, total - most), min(most, total - 1) + 1)
        return jnp.stack([one, total - one])
    sizes = jnp.asarray(profile(number_of, total, most, slope), jnp.int32)
    twos = (number_of - 1) // 2
    giver, sink = sizes[1:1 + 2 * twos:2], sizes[2:2 + 2 * twos:2]
    margin = jnp.minimum(giver - 1, most - sink)
    shifted = jax.random.randint(jax.random.fold_in(stream_key, 1), (twos,), 0, 1 << 20) % (margin + 1)
    sizes = sizes.at[1:1 + 2 * twos:2].set(giver - shifted).at[2:2 + 2 * twos:2].set(sink + shifted)
    return sizes[jax.random.permutation(jax.random.fold_in(stream_key, 2), number_of)]


def normal_values(rng, dims, deviation, reach, shards=(), held_as=jnp.bfloat16):
    gain = steps_of(rng, dims, shards, -0.22, 0.18) if shards else 1.0
    entries = jax.random.normal(rng, dims, jnp.float32) * deviation * gain
    return jnp.minimum(jnp.maximum(entries, -reach), reach).astype(held_as)


def setup_inputs(seed: int = 0) -> dict:
    keys = jax.random.split(jax.random.key(seed), 8)
    q_latent = normal_values(keys[0], (GROUPS, REQUESTS_GROUP, DRAFT, QL), 1.0, 6.0, ((1, 32),))
    draft_start = plant(jax.random.randint(keys[1], (GROUPS, REQUESTS_GROUP), CTX, 2 * CTX), jax.random.fold_in(keys[1], 1), CTX, (2 * CTX) - 1).astype(jnp.int32)
    cache_len = jax.vmap(lambda own: ragged_sizes(own, REQUESTS_GROUP, REQUESTS_GROUP * (CTX - DRAFT) * 5 // 8, CTX - DRAFT, 2))(jax.random.split(keys[2], GROUPS)).reshape((GROUPS, REQUESTS_GROUP)).astype(jnp.int32)
    latent_cache = draw_latent_cache(jax.random.fold_in(keys[7], 71), 0)
    w_q_up = normal_values(keys[4], (QL, HEADS * (NOPE + ROPE)), QL ** -0.5, 0.15625, ((1, 32),))
    w_k_absorb = normal_values(keys[5], (HEADS, NOPE, KVL), NOPE ** -0.5, 0.5, ((0, 32),))
    value_up_weight = normal_values(keys[6], (HEADS, KVL, VD), KVL ** -0.5, 0.25, ((0, 32),))
    return {"q_latent": q_latent, "draft_start": draft_start, "cache_len": cache_len, "latent_cache": latent_cache, "w_q_up": w_q_up, "w_k_absorb": w_k_absorb, "value_up_weight": value_up_weight}


def turn_rotary(query_rope, positions):
    half_width = ROPE // 2
    freqs = 10000.0 ** (-jnp.arange(half_width).astype(jnp.float32) * 2.0 / ROPE)
    angles = positions.astype(jnp.float32)[:, :, None, None] * freqs
    cosine = jnp.cos(angles)
    sine_table = jnp.sin(angles)
    first_half = query_rope[..., :half_width]
    second_half = query_rope[..., half_width:]
    return jnp.concatenate([first_half * cosine - second_half * sine_table, second_half * cosine + first_half * sine_table], axis=-1)


def reference(q_latent, draft_start, cache_len, latent_cache, w_q_up, w_k_absorb, value_up_weight):
    requests = GROUPS * REQUESTS_GROUP
    head_dim = NOPE + ROPE
    flat_rows = q_latent.reshape(requests * DRAFT, QL)
    q_full = jnp.dot(flat_rows, w_q_up, preferred_element_type=jnp.float32).astype(jnp.bfloat16)
    q_full = q_full.reshape(requests, DRAFT, HEADS, head_dim)
    query_nope = q_full[..., :NOPE].astype(jnp.float32)
    query_rope = q_full[..., NOPE:].astype(jnp.float32)
    absorbed = jnp.einsum("rdhn,hnk->rdhk", query_nope, w_k_absorb.astype(jnp.float32), precision=lax.Precision.HIGHEST)
    positions = draft_start.reshape(requests)[:, None] + jnp.arange(DRAFT).astype(jnp.int32)[None, :]
    rotated_rows = turn_rotary(query_rope, positions)
    query = jnp.concatenate([absorbed, rotated_rows], axis=-1).astype(jnp.bfloat16)
    caches = latent_cache.reshape(requests, CTX, KVL + ROPE)
    lengths = cache_len.reshape(requests)
    scale = float(head_dim) ** -0.5

    def one_request(packed):
        request_query, cache, length = packed
        query_matrix = request_query.reshape(DRAFT * HEADS, KVL + ROPE).astype(jnp.float32)
        cache_f = cache.astype(jnp.float32)
        scores = jnp.dot(query_matrix, cache_f.T, precision=lax.Precision.HIGHEST)
        scores = scores.reshape(DRAFT, HEADS, CTX) * scale
        slots = jnp.arange(CTX).astype(jnp.int32)
        limit = length + jnp.arange(DRAFT).astype(jnp.int32)
        visible = slots[None, None, :] <= limit[:, None, None]
        peak = jnp.max(jnp.where(visible, scores, -jnp.inf), axis=2, keepdims=True)
        expo = jnp.where(visible, jnp.exp(scores - peak), 0.0)
        probs = (expo / jnp.sum(expo, axis=2, keepdims=True)).astype(jnp.bfloat16)
        latent_output = jnp.dot(probs.reshape(DRAFT * HEADS, CTX).astype(jnp.float32), cache_f[:, :KVL], precision=lax.Precision.HIGHEST)
        return latent_output.astype(jnp.bfloat16).reshape(DRAFT, HEADS, KVL)

    latent_output = lax.map(one_request, (query, caches, lengths))
    values = jnp.einsum("aofu,fub->aofb", latent_output.astype(jnp.float32), value_up_weight.astype(jnp.float32), precision=lax.Precision.HIGHEST)
    return values.astype(jnp.bfloat16).reshape(GROUPS, REQUESTS_GROUP, DRAFT, HEADS * VD)
```

```python
import functools
import math
import jax
import jax.numpy as jnp
from jax import lax
from jax.experimental import pallas as pl
from jax.experimental.pallas import tpu as pltpu
from jax.sharding import PartitionSpec as P

MESH = pl.DeviceIdType.MESH


def spread_step(count):
    step = max(1, int(count * 0.41))
    while math.gcd(step, count) != 1:
        step += 1
    return step


def rotary_tables(draft_start, drafts, heads_here, rope_width):
    half = rope_width // 2
    freqs = 10000.0 ** (-jnp.arange(half).astype(jnp.float32) * 2.0 / rope_width)
    positions = draft_start[None, :] + lax.iota(jnp.int32, drafts)[:, None]
    angles = positions.astype(jnp.float32)[:, :, None] * freqs
    cosine, sine = jnp.cos(angles), jnp.sin(angles)
    owned = draft_start.shape[0]

    def spread(low, high):
        both = jnp.concatenate([low, high], axis=-1).reshape(drafts, 1, owned * rope_width)
        both = jnp.broadcast_to(both, (drafts, heads_here, owned * rope_width))
        return both.reshape(drafts * heads_here, owned * rope_width)

    return spread(cosine, cosine), spread(-sine, sine)


def attend(which, length, query, cache, scores, peak_part, sum_part, acc, drafts, group, kv, coef, chunk):
    rows = query.shape[0]
    ctx = cache.shape[1]
    lanes = peak_part.shape[1]
    row = lax.broadcasted_iota(jnp.int32, (rows, 1), 0)
    limit = length + lax.rem(row, group) // (group // drafts)
    peak_part[...] = jnp.full_like(peak_part, -jnp.inf)
    sum_part[...] = jnp.zeros_like(sum_part)
    acc[...] = jnp.zeros_like(acc)

    def fold(part, op):
        out = part[:, :lanes]
        for at in range(lanes, chunk, lanes):
            out = op(out, part[:, at:at + lanes])
        return out

    def score(step, carry):
        base = pl.multiple_of(step * chunk, chunk)
        part = lax.dot_general(
            query[...], cache[which, pl.ds(base, chunk), :], (((1,), (1,)), ((), ())),
            preferred_element_type=jnp.float32,
        )
        slot = base + lax.broadcasted_iota(jnp.int32, (1, chunk), 1)
        part = jnp.where(slot <= limit, part, -jnp.inf)
        scores[:, pl.ds(base, chunk)] = part
        peak_part[...] = jnp.maximum(peak_part[...], fold(part, jnp.maximum))
        return carry

    lax.fori_loop(0, ctx // chunk, score, 0)
    peak = jnp.max(peak_part[...], axis=1, keepdims=True) * coef

    def expo(step, carry):
        base = pl.multiple_of(step * chunk, chunk)
        part = jnp.exp2(scores[:, pl.ds(base, chunk)] * coef - peak)
        scores[:, pl.ds(base, chunk)] = part
        sum_part[...] += fold(part, jnp.add)
        return carry

    lax.fori_loop(0, ctx // chunk, expo, 0)
    inverse = 1.0 / jnp.sum(sum_part[...], axis=1, keepdims=True)

    def weigh(step, carry):
        base = pl.multiple_of(step * chunk, chunk)
        probs = (scores[:, pl.ds(base, chunk)] * inverse).astype(jnp.bfloat16)
        acc[...] += jnp.dot(
            probs, cache[which, pl.ds(base, chunk), :kv], preferred_element_type=jnp.float32
        )
        return carry

    lax.fori_loop(0, ctx // chunk, weigh, 0)


def kernel(
    n, drafts, heads_here, nope, rope, kv, vd, coef, chunk,
    length_ref, latent_ref, cos_ref, sin_ref, cache_hbm, wq_hbm, wk_hbm, wv_hbm,
    out_ref,
    cache, wq, wk, wv, q_full, wide_f32, rope_f32, send_q, send_r, recv_q, recv_r,
    query, scores, peak_part, sum_part, acc, send_o, recv_o,
    cache_sem, wq_sem, wk_sem, wv_sem, own_sem,
    sq_sem, sr_sem, so_sem, rq_sem, rr_sem, ro_sem,
):
    me = lax.axis_index("wide")
    owned = cache.shape[0]
    group = drafts * heads_here
    head_dim = nope + rope
    step = spread_step(n)

    def partner(t):
        return lax.rem(me + lax.rem(t * step, n), n)

    load_q = pltpu.make_async_copy(wq_hbm, wq, wq_sem)
    load_k = pltpu.make_async_copy(wk_hbm, wk, wk_sem)
    load_v = pltpu.make_async_copy(wv_hbm, wv, wv_sem)
    loads = [
        pltpu.make_async_copy(cache_hbm.at[which], cache.at[which], cache_sem.at[which])
        for which in range(owned)
    ]
    load_q.start()
    load_k.start()
    for load in loads:
        load.start()
    load_v.start()

    barrier = pltpu.get_barrier_semaphore()

    def greet(t, carry):
        pl.semaphore_signal(barrier, inc=1, device_id={"wide": partner(t)}, device_id_type=MESH)
        return carry

    lax.fori_loop(1, n, greet, 0)

    load_q.wait()
    columns = heads_here * head_dim
    block = 256 if columns % 256 == 0 else columns
    for at in range(0, columns, block):
        part = jnp.dot(latent_ref[...], wq[:, at:at + block], preferred_element_type=jnp.float32)
        q_full[:, at:at + block] = part.astype(jnp.bfloat16).astype(jnp.float32)
    load_k.wait()
    rows = q_full.shape[0]
    for head in range(heads_here):
        at = head * head_dim
        absorbed = jnp.dot(
            q_full[:, at:at + nope].astype(jnp.bfloat16), wk[head],
            preferred_element_type=jnp.float32,
        )
        for part in range(kv // 128):
            wide_f32[part, pl.ds(head, rows, stride=heads_here), :] = absorbed[:, part * 128:part * 128 + 128]
        tail = q_full[:, at + nope:at + head_dim]
        rope_f32[pl.ds(head, rows, stride=heads_here), :] = jnp.concatenate([tail] * owned, axis=-1)
    for part in range(kv // 128):
        packed = wide_f32[part].astype(jnp.bfloat16).reshape(n, owned, group, 128)
        for which in range(owned):
            send_q[which, :, :, part * 128:part * 128 + 128] = packed[:, which]
    turned = rope_f32[:, :rope].reshape(n, owned, group, rope)
    send_r[...] = jnp.concatenate(
        [turned[:, which] for which in range(owned)], axis=-1
    ).astype(jnp.bfloat16)

    pl.semaphore_wait(barrier, n - 1)

    def post(t, carry, which):
        d = partner(t)
        if which == 0:
            pltpu.make_async_remote_copy(
                src_ref=send_r.at[d], dst_ref=recv_r.at[me], send_sem=sr_sem, recv_sem=rr_sem,
                device_id={"wide": d}, device_id_type=MESH,
            ).start()
        pltpu.make_async_remote_copy(
            src_ref=send_q.at[which, d], dst_ref=recv_q.at[which, me],
            send_sem=sq_sem.at[which], recv_sem=rq_sem.at[which],
            device_id={"wide": d}, device_id_type=MESH,
        ).start()
        return carry

    for which in range(owned):
        lax.fori_loop(1, n, functools.partial(post, which=which), 0)
        own = pltpu.make_async_copy(send_q.at[which, me], recv_q.at[which, me], own_sem)
        own.start()
        own.wait()
    own = pltpu.make_async_copy(send_r.at[me], recv_r.at[me], own_sem)
    own.start()
    own.wait()

    def all_but_one(ref, sem):
        pltpu.make_async_copy(ref.at[pl.ds(0, n - 1)], ref.at[pl.ds(0, n - 1)], sem).wait()

    def post_out(t, carry, which):
        d = partner(t)
        pltpu.make_async_remote_copy(
            src_ref=send_o.at[which, d], dst_ref=recv_o.at[which, me],
            send_sem=so_sem.at[which], recv_sem=ro_sem.at[which],
            device_id={"wide": d}, device_id_type=MESH,
        ).start()
        return carry

    all_but_one(recv_r, rr_sem)
    turn = recv_r[...].astype(jnp.float32)
    width = turn.shape[2]
    flat = turn.reshape(n * group, width)
    lane = lax.broadcasted_iota(jnp.int32, (1, width), 1)
    half = rope // 2
    swapped = jnp.where(
        lax.rem(lane, rope) < half,
        pltpu.roll(flat, width - half, 1),
        pltpu.roll(flat, half, 1),
    ).reshape(n, group, width)
    rotated = (turn * cos_ref[...][None] + swapped * sin_ref[...][None]).reshape(n * group, width)
    rope_f32[:n * group, :] = rotated

    for which in range(owned):
        all_but_one(recv_q.at[which], rq_sem.at[which])
        query[:, :kv] = recv_q[which].reshape(n * group, kv)
        query[:, kv:] = rope_f32[:n * group, which * rope:(which + 1) * rope].astype(jnp.bfloat16)
        loads[which].wait()
        attend(
            which, length_ref[which], query, cache, scores, peak_part, sum_part, acc,
            drafts, group, kv, coef, chunk,
        )
        send_o[which] = acc[...].astype(jnp.bfloat16).reshape(n, group, kv)
        lax.fori_loop(1, n, functools.partial(post_out, which=which), 0)
        own = pltpu.make_async_copy(send_o.at[which, me], recv_o.at[which, me], own_sem)
        own.start()
        own.wait()

    load_v.wait()
    for which in range(owned):
        all_but_one(recv_o.at[which], ro_sem.at[which])
    for part in range(kv // 128):
        lanes = slice(part * 128, part * 128 + 128)
        arrived = jnp.stack([recv_o[which, :, :, lanes] for which in range(owned)], axis=1)
        wide_f32[part] = arrived.astype(jnp.float32).reshape(n * owned * group, 128)
    for head in range(heads_here):
        mine = jnp.concatenate(
            [wide_f32[part, pl.ds(head, rows, stride=heads_here), :] for part in range(kv // 128)], axis=-1
        ).astype(jnp.bfloat16)
        out_ref[:, head * vd:(head + 1) * vd] = jnp.dot(
            mine, wv[head], preferred_element_type=jnp.float32
        ).astype(jnp.bfloat16)

    all_but_one(send_r, sr_sem)
    for which in range(owned):
        all_but_one(send_q.at[which], sq_sem.at[which])
        all_but_one(send_o.at[which], so_sem.at[which])


def per_device(q_latent, draft_start, cache_len, latent_cache, w_q_up, w_k_absorb, value_up_weight):
    n = lax.axis_size("wide")
    heads_here, nope, kv = w_k_absorb.shape
    vd = value_up_weight.shape[2]
    head_dim = w_q_up.shape[1] // heads_here
    rope = head_dim - nope
    owned, ctx, width = latent_cache.shape[1:]
    drafts, ql = q_latent.shape[2:]
    group = drafts * heads_here
    rows = n * owned * drafts
    chunk = min(512, ctx)
    coef = float(head_dim) ** -0.5 * math.log2(math.e)
    bf16, f32 = jnp.bfloat16, jnp.float32

    latent = lax.all_gather(q_latent[0], "wide", axis=0, tiled=True).reshape(rows, ql)
    wq = lax.all_gather(w_q_up, "batch", axis=0, tiled=True)
    cosine, sine = rotary_tables(draft_start[0], drafts, heads_here, rope)

    vmem = pl.BlockSpec(memory_space=pltpu.VMEM)
    hbm = pl.BlockSpec(memory_space=pl.ANY)
    dma = pltpu.SemaphoreType.DMA
    out = pl.pallas_call(
        functools.partial(kernel, n, drafts, heads_here, nope, rope, kv, vd, coef, chunk),
        out_shape=jax.ShapeDtypeStruct((rows, heads_here * vd), bf16),
        in_specs=[pl.BlockSpec(memory_space=pltpu.SMEM), vmem, vmem, vmem, hbm, hbm, hbm, hbm],
        out_specs=vmem,
        scratch_shapes=[
            pltpu.VMEM((owned, ctx, width), bf16),
            pltpu.VMEM(wq.shape, bf16),
            pltpu.VMEM(w_k_absorb.shape, bf16),
            pltpu.VMEM(value_up_weight.shape, bf16),
            pltpu.VMEM((rows, heads_here * head_dim), f32),
            pltpu.VMEM((kv // 128, rows * heads_here, 128), f32),
            pltpu.VMEM((rows * heads_here, owned * rope), f32),
            pltpu.VMEM((owned, n, group, kv), bf16),
            pltpu.VMEM((n, group, owned * rope), bf16),
            pltpu.VMEM((owned, n, group, kv), bf16),
            pltpu.VMEM((n, group, owned * rope), bf16),
            pltpu.VMEM((n * group, width), bf16),
            pltpu.VMEM((n * group, ctx), f32),
            pltpu.VMEM((n * group, min(128, chunk)), f32),
            pltpu.VMEM((n * group, min(128, chunk)), f32),
            pltpu.VMEM((n * group, kv), f32),
            pltpu.VMEM((owned, n, group, kv), bf16),
            pltpu.VMEM((owned, n, group, kv), bf16),
            dma((owned,)), dma, dma, dma, dma,
            dma((owned,)), dma, dma((owned,)), dma((owned,)), dma, dma((owned,)),
        ],
        compiler_params=pltpu.CompilerParams(
            collective_id=0, has_side_effects=True, vmem_limit_bytes=56 << 20
        ),
    )(cache_len[0], latent, cosine, sine, latent_cache[0], wq, w_k_absorb, value_up_weight)
    return out.reshape(1, n * owned, drafts, heads_here * vd)


def solution(mesh):
    in_specs = (
        P("batch", "wide", None, None),
        P("batch", "wide"),
        P("batch", "wide"),
        P("batch", "wide", None, None),
        P("batch", "wide"),
        P("wide", None, None),
        P("wide", None, None),
    )
    out_specs = P("batch", None, None, "wide")
    return jax.shard_map(
        per_device, mesh=mesh, in_specs=in_specs, out_specs=out_specs, check_vma=False
    )
```

```python
import functools
import math
import jax
import jax.numpy as jnp
from jax import lax
from jax.experimental import pallas as pl
from jax.experimental.pallas import tpu as pltpu
from jax.sharding import PartitionSpec as P

MESH = pl.DeviceIdType.MESH


def spread_step(count):
    step = max(1, int(count * 0.41))
    while math.gcd(step, count) != 1:
        step += 1
    return step


def rotary_tables(start_ref, freq, drafts, group, rope_width, owned):
    shape = (group, owned * rope_width)
    row = lax.broadcasted_iota(jnp.int32, shape, 0) // (group // drafts)
    lane = lax.broadcasted_iota(jnp.int32, shape, 1)
    start = jnp.full(shape, start_ref[0], jnp.int32)
    for which in range(1, owned):
        start = jnp.where(lane // rope_width == which, start_ref[which], start)
    angle = (start + row).astype(jnp.float32) * freq
    turns = jnp.floor(angle * (0.5 / math.pi) + 0.5)
    angle = angle - turns * 6.28125
    angle = angle - turns * 0.0019340515136718750
    angle = angle - turns * 1.2556659146475769e-06
    sine = jnp.sin(angle)
    sine = jnp.where(lax.rem(lane, rope_width) < rope_width // 2, -sine, sine)
    return jnp.cos(angle), sine


def attend(which, length, query, cache, scores, peak_part, sum_part, acc, drafts, group, kv, coef, chunk):
    rows = query.shape[0]
    ctx = cache.shape[2]
    lanes = peak_part.shape[1]
    row = lax.broadcasted_iota(jnp.int32, (rows, 1), 0)
    limit = length + lax.rem(row, group) // (group // drafts)
    peak_part[...] = jnp.full_like(peak_part, -jnp.inf)
    sum_part[...] = jnp.zeros_like(sum_part)
    acc[...] = jnp.zeros_like(acc)

    def fold(part, op):
        out = part[:, :lanes]
        for at in range(lanes, chunk, lanes):
            out = op(out, part[:, at:at + lanes])
        return out

    def score(step, carry):
        base = pl.multiple_of(step * chunk, chunk)
        part = lax.dot_general(
            query[...], cache[which, :, pl.ds(base, chunk)], (((1,), (0,)), ((), ())),
            preferred_element_type=jnp.float32,
        )
        slot = base + lax.broadcasted_iota(jnp.int32, (1, chunk), 1)
        part = jnp.where(slot <= limit, part, -jnp.inf)
        scores[:, pl.ds(base, chunk)] = part
        peak_part[...] = jnp.maximum(peak_part[...], fold(part, jnp.maximum))
        return carry

    lax.fori_loop(0, ctx // chunk, score, 0)
    peak = jnp.max(peak_part[...], axis=1, keepdims=True) * coef

    def expo(step, carry):
        base = pl.multiple_of(step * chunk, chunk)
        part = jnp.exp2(scores[:, pl.ds(base, chunk)] * coef - peak)
        scores[:, pl.ds(base, chunk)] = part
        sum_part[...] += fold(part, jnp.add)
        return carry

    lax.fori_loop(0, ctx // chunk, expo, 0)
    inverse = 1.0 / jnp.sum(sum_part[...], axis=1, keepdims=True)

    def weigh(step, carry):
        base = pl.multiple_of(step * chunk, chunk)
        probs = (scores[:, pl.ds(base, chunk)] * inverse).astype(jnp.bfloat16)
        acc[...] += lax.dot_general(
            probs, cache[which, :kv, pl.ds(base, chunk)], (((1,), (1,)), ((), ())),
            preferred_element_type=jnp.float32,
        )
        return carry

    lax.fori_loop(0, ctx // chunk, weigh, 0)


def kernel(
    n, drafts, heads_here, nope, rope, kv, vd, coef, chunk,
    length_ref, start_ref, latent_ref, freq_ref, cache_hbm, wq_hbm, wk_hbm, wv_hbm,
    out_ref,
    cache, wq, wk, wv, gather, own_f32, q_full, wide_f32, rope_f32, send_q, send_r, recv_q, recv_r,
    query, scores, peak_part, sum_part, acc, send_o, recv_o,
    cache_sem, wq_sem, wk_sem, wv_sem, own_sem, ga_sem, gb_sem, gc_sem, ha_sem, hb_sem, hc_sem,
    sq_sem, sr_sem, so_sem, rq_sem, rr_sem, ro_sem,
):
    me = lax.axis_index("wide")
    owned = cache.shape[0]
    group = drafts * heads_here
    head_dim = nope + rope
    cores, lines, plane = gather.shape[:3]
    spots = lines * plane
    core, spot = lax.rem(me, cores), me // cores
    line, place = spot // plane, lax.rem(spot, plane)
    other = cores - 1 - core
    step, spot_step = spread_step(n), spread_step(spots)

    def partner(t):
        return lax.rem(me + lax.rem(t * step, n), n)

    load_q = pltpu.make_async_copy(wq_hbm, wq, wq_sem)
    load_k = pltpu.make_async_copy(wk_hbm, wk, wk_sem)
    load_v = pltpu.make_async_copy(wv_hbm, wv, wv_sem)
    loads = [
        pltpu.make_async_copy(cache_hbm.at[which], cache.at[which], cache_sem.at[which])
        for which in range(owned)
    ]
    barrier = pltpu.get_barrier_semaphore()

    def greet(t, carry):
        pl.semaphore_signal(barrier, inc=1, device_id={"wide": partner(t)}, device_id_type=MESH)
        return carry

    lax.fori_loop(1, n, greet, 0)
    load_q.start()
    load_k.start()
    for load in loads:
        load.start()
    load_v.start()

    for which in range(owned):
        own_f32[which * drafts:(which + 1) * drafts, :] = latent_ref[which].astype(jnp.float32)
    mine = own_f32[...]
    depth = mine.shape[1] // 2
    stacked = jnp.concatenate([mine[:, :depth], mine[:, depth:]], axis=0)
    gather[core, line, place] = stacked.astype(jnp.bfloat16)
    cosine, sine = rotary_tables(start_ref, freq_ref[...], drafts, group, rope, owned)
    pl.semaphore_wait(barrier, n - 1)

    def to_line(t, carry):
        there = lax.rem(line + t, lines)
        mine = gather.at[core, line, place]
        pltpu.make_async_remote_copy(
            src_ref=mine, dst_ref=mine, send_sem=ga_sem, recv_sem=ha_sem,
            device_id={"wide": (there * plane + place) * cores + core}, device_id_type=MESH,
        ).start()
        return carry

    def to_plane(t, carry):
        there = lax.rem(place + t, plane)
        mine = gather.at[core, :, place]
        pltpu.make_async_remote_copy(
            src_ref=mine, dst_ref=mine, send_sem=gb_sem, recv_sem=hb_sem,
            device_id={"wide": (line * plane + there) * cores + core}, device_id_type=MESH,
        ).start()
        return carry

    def landed(ref, sem):
        pltpu.make_async_copy(ref, ref, sem).wait()

    lax.fori_loop(1, lines, to_line, 0)
    landed(gather.at[core, pl.ds(0, lines - 1), place], ha_sem)
    lax.fori_loop(1, plane, to_plane, 0)
    landed(gather.at[core, :, pl.ds(0, plane - 1)], hb_sem)
    across = pltpu.make_async_remote_copy(
        src_ref=gather.at[core], dst_ref=gather.at[core], send_sem=gc_sem, recv_sem=hc_sem,
        device_id={"wide": spot * cores + other}, device_id_type=MESH,
    )
    across.start()

    def queries(side):
        rows = q_full.shape[0]
        latents = gather[side].reshape(spots, 2 * owned * drafts, depth).astype(jnp.float32)
        low = latents[:, :owned * drafts].reshape(rows, depth).astype(jnp.bfloat16)
        high = latents[:, owned * drafts:].reshape(rows, depth).astype(jnp.bfloat16)
        columns = heads_here * head_dim
        block = 256 if columns % 256 == 0 else columns
        for at in range(0, columns, block):
            part = jnp.dot(low, wq[:depth, at:at + block], preferred_element_type=jnp.float32)
            part += jnp.dot(high, wq[depth:, at:at + block], preferred_element_type=jnp.float32)
            q_full[:, at:at + block] = part.astype(jnp.bfloat16).astype(jnp.float32)
        for head in range(heads_here):
            at = head * head_dim
            absorbed = jnp.dot(
                q_full[:, at:at + nope].astype(jnp.bfloat16), wk[head],
                preferred_element_type=jnp.float32,
            )
            for part in range(kv // 128):
                wide_f32[part, pl.ds(head, rows, stride=heads_here), :] = absorbed[:, part * 128:part * 128 + 128]
            tail = q_full[:, at + nope:at + head_dim]
            rope_f32[pl.ds(head, rows, stride=heads_here), :] = jnp.concatenate([tail] * owned, axis=-1)
        for part in range(kv // 128):
            packed = wide_f32[part, :rows * heads_here].astype(jnp.bfloat16).reshape(spots, owned, group, 128)
            for which in range(owned):
                send_q[side, which, :, :, part * 128:part * 128 + 128] = packed[:, which]
        turned = rope_f32[:, :rope].reshape(spots, owned, group, rope)
        send_r[side] = jnp.concatenate(
            [turned[:, which] for which in range(owned)], axis=-1
        ).astype(jnp.bfloat16)

    def post(t, carry, which, side):
        there = lax.rem(spot + lax.rem(t * spot_step, spots), spots)
        target = {"wide": there * cores + side}
        if which == 0:
            pltpu.make_async_remote_copy(
                src_ref=send_r.at[side, there], dst_ref=recv_r.at[me], send_sem=sr_sem, recv_sem=rr_sem,
                device_id=target, device_id_type=MESH,
            ).start()
        pltpu.make_async_remote_copy(
            src_ref=send_q.at[side, which, there], dst_ref=recv_q.at[which, me],
            send_sem=sq_sem.at[which], recv_sem=rq_sem.at[which],
            device_id=target, device_id_type=MESH,
        ).start()
        return carry

    load_q.wait()
    load_k.wait()
    queries(core)
    lax.fori_loop(1, spots, functools.partial(post, which=0, side=core), 0)
    across.wait_recv()
    queries(other)
    lax.fori_loop(0, spots, functools.partial(post, which=0, side=other), 0)
    for which in range(1, owned):
        lax.fori_loop(1, spots, functools.partial(post, which=which, side=core), 0)
        lax.fori_loop(0, spots, functools.partial(post, which=which, side=other), 0)
    keep = [
        pltpu.make_async_copy(send_q.at[core, which, spot], recv_q.at[which, me], own_sem.at[which])
        for which in range(owned)
    ] + [pltpu.make_async_copy(send_r.at[core, spot], recv_r.at[me], own_sem.at[owned])]
    for copy in keep:
        copy.start()
    for copy in keep:
        copy.wait()

    def all_but_one(ref, sem):
        pltpu.make_async_copy(ref.at[pl.ds(0, n - 1)], ref.at[pl.ds(0, n - 1)], sem).wait()

    def post_out(t, carry, which):
        d = partner(t)
        pltpu.make_async_remote_copy(
            src_ref=send_o.at[which, d], dst_ref=recv_o.at[which, me],
            send_sem=so_sem.at[which], recv_sem=ro_sem.at[which],
            device_id={"wide": d}, device_id_type=MESH,
        ).start()
        return carry

    all_but_one(recv_r, rr_sem)
    turn = recv_r[...].astype(jnp.float32)
    width = turn.shape[2]
    flat = turn.reshape(n * group, width)
    lane = lax.broadcasted_iota(jnp.int32, (1, width), 1)
    half = rope // 2
    swapped = jnp.where(
        lax.rem(lane, rope) < half,
        pltpu.roll(flat, width - half, 1),
        pltpu.roll(flat, half, 1),
    ).reshape(n, group, width)
    rotated = (turn * cosine[None] + swapped * sine[None]).reshape(n * group, width)
    rope_f32[:n * group, :] = rotated

    for which in range(owned):
        all_but_one(recv_q.at[which], rq_sem.at[which])
        query[:, :kv] = recv_q[which].reshape(n * group, kv)
        query[:, kv:] = rope_f32[:n * group, which * rope:(which + 1) * rope].astype(jnp.bfloat16)
        loads[which].wait()
        attend(
            which, length_ref[which], query, cache, scores, peak_part, sum_part, acc,
            drafts, group, kv, coef, chunk,
        )
        send_o[which] = acc[...].astype(jnp.bfloat16).reshape(n, group, kv)
        lax.fori_loop(1, n, functools.partial(post_out, which=which), 0)
        own = pltpu.make_async_copy(send_o.at[which, me], recv_o.at[which, me], own_sem.at[0])
        own.start()
        own.wait()

    load_v.wait()
    rows = out_ref.shape[0]
    for which in range(owned):
        all_but_one(recv_o.at[which], ro_sem.at[which])
    for part in range(kv // 128):
        lanes = slice(part * 128, part * 128 + 128)
        arrived = jnp.stack([recv_o[which, :, :, lanes] for which in range(owned)], axis=1)
        wide_f32[part] = arrived.astype(jnp.float32).reshape(n * owned * group, 128)
    for head in range(heads_here):
        mine = jnp.concatenate(
            [wide_f32[part, pl.ds(head, rows, stride=heads_here), :] for part in range(kv // 128)], axis=-1
        ).astype(jnp.bfloat16)
        out_ref[:, head * vd:(head + 1) * vd] = jnp.dot(
            mine, wv[head], preferred_element_type=jnp.float32
        ).astype(jnp.bfloat16)

    landed(gather.at[core, pl.ds(0, lines - 1), place], ga_sem)
    landed(gather.at[core, :, pl.ds(0, plane - 1)], gb_sem)
    across.wait_send()
    all_but_one(recv_r, sr_sem)
    for which in range(owned):
        all_but_one(recv_q.at[which], sq_sem.at[which])
        all_but_one(send_o.at[which], so_sem.at[which])


def per_device(q_latent, draft_start, cache_len, latent_cache, w_q_up, w_k_absorb, value_up_weight):
    n = lax.axis_size("wide")
    heads_here, nope, kv = w_k_absorb.shape
    vd = value_up_weight.shape[2]
    head_dim = w_q_up.shape[1] // heads_here
    rope = head_dim - nope
    owned, ctx, width = latent_cache.shape[1:]
    drafts, ql = q_latent.shape[2:]
    group = drafts * heads_here
    rows = n * owned * drafts
    chunk = min(512, ctx)
    coef = float(head_dim) ** -0.5 * math.log2(math.e)
    bf16, f32 = jnp.bfloat16, jnp.float32

    wq = lax.all_gather(w_q_up, "batch", axis=0, tiled=True)
    freqs = 10000.0 ** (-jnp.arange(rope // 2).astype(f32) * 2.0 / rope)
    freqs = jnp.tile(freqs, 2 * owned)[None]
    cores, plane = 2, 4
    spots, lines = n // cores, n // (cores * plane)

    vmem = pl.BlockSpec(memory_space=pltpu.VMEM)
    smem = pl.BlockSpec(memory_space=pltpu.SMEM)
    hbm = pl.BlockSpec(memory_space=pl.ANY)
    dma = pltpu.SemaphoreType.DMA
    out = pl.pallas_call(
        functools.partial(kernel, n, drafts, heads_here, nope, rope, kv, vd, coef, chunk),
        out_shape=jax.ShapeDtypeStruct((rows, heads_here * vd), bf16),
        in_specs=[smem, smem, vmem, vmem, hbm, hbm, hbm, hbm],
        out_specs=vmem,
        scratch_shapes=[
            pltpu.VMEM((owned, width, ctx), bf16),
            pltpu.VMEM(wq.shape, bf16),
            pltpu.VMEM(w_k_absorb.shape, bf16),
            pltpu.VMEM(value_up_weight.shape, bf16),
            pltpu.VMEM((cores, lines, plane, 2 * owned * drafts, ql // 2), bf16),
            pltpu.VMEM((owned * drafts, ql), f32),
            pltpu.VMEM((rows // cores, heads_here * head_dim), f32),
            pltpu.VMEM((kv // 128, rows * heads_here, 128), f32),
            pltpu.VMEM((rows * heads_here // cores, owned * rope), f32),
            pltpu.VMEM((cores, owned, spots, group, kv), bf16),
            pltpu.VMEM((cores, spots, group, owned * rope), bf16),
            pltpu.VMEM((owned, n, group, kv), bf16),
            pltpu.VMEM((n, group, owned * rope), bf16),
            pltpu.VMEM((n * group, width), bf16),
            pltpu.VMEM((n * group, ctx), f32),
            pltpu.VMEM((n * group, min(128, chunk)), f32),
            pltpu.VMEM((n * group, min(128, chunk)), f32),
            pltpu.VMEM((n * group, kv), f32),
            pltpu.VMEM((owned, n, group, kv), bf16),
            pltpu.VMEM((owned, n, group, kv), bf16),
            dma((owned,)), dma, dma, dma, dma((owned + 1,)), dma, dma, dma, dma, dma, dma,
            dma((owned,)), dma, dma((owned,)), dma((owned,)), dma, dma((owned,)),
        ],
        compiler_params=pltpu.CompilerParams(
            collective_id=0, has_side_effects=True, vmem_limit_bytes=56 << 20
        ),
    )(cache_len[0], draft_start[0], q_latent[0], freqs, jnp.swapaxes(latent_cache[0], 1, 2), wq, w_k_absorb, value_up_weight)
    return out.reshape(1, n * owned, drafts, heads_here * vd)


def solution(mesh):
    in_specs = (
        P("batch", "wide", None, None),
        P("batch", "wide"),
        P("batch", "wide"),
        P("batch", "wide", None, None),
        P("batch", "wide"),
        P("wide", None, None),
        P("wide", None, None),
    )
    out_specs = P("batch", None, None, "wide")
    return jax.shard_map(
        per_device, mesh=mesh, in_specs=in_specs, out_specs=out_specs, check_vma=False
    )
```

```python
import functools
import math
import jax
import jax.numpy as jnp
import numpy as np
from jax import lax
from jax.experimental import pallas as pl
from jax.experimental.pallas import tpu as pltpu
from jax.sharding import PartitionSpec as P

MESH = pl.DeviceIdType.MESH


def spread_step(count):
    step = max(1, int(count * 0.41))
    while math.gcd(step, count) != 1:
        step += 1
    return step


def rotary_tables(start_ref, drafts, group, rope_width, owned):
    shape = (group, owned * rope_width)
    row = lax.broadcasted_iota(jnp.int32, shape, 0) // (group // drafts)
    lane = lax.broadcasted_iota(jnp.int32, shape, 1)
    half = rope_width // 2
    freqs = 10000.0 ** (-np.arange(half) * 2.0 / rope_width)
    freq = jnp.zeros(shape, jnp.float32)
    for at in range(half):
        freq = jnp.where(lax.rem(lane, half) == at, np.float32(freqs[at]), freq)
    start = jnp.full(shape, start_ref[0], jnp.int32)
    for which in range(1, owned):
        start = jnp.where(lane // rope_width == which, start_ref[which], start)
    angle = (start + row).astype(jnp.float32) * freq
    turns = jnp.floor(angle * (0.5 / math.pi) + 0.5)
    angle = angle - turns * 6.28125
    angle = angle - turns * 0.0019340515136718750
    angle = angle - turns * 1.2556659146475769e-06
    sine = jnp.sin(angle)
    sine = jnp.where(lax.rem(lane, rope_width) < rope_width // 2, -sine, sine)
    return jnp.cos(angle), sine


def attend(which, length, query, cache, scores, peak_part, sum_part, acc, drafts, group, kv, coef, chunk):
    rows = query.shape[0]
    ctx = cache.shape[2]
    lanes = peak_part.shape[1]
    row = lax.broadcasted_iota(jnp.int32, (rows, 1), 0)
    limit = length + lax.rem(row, group) // (group // drafts)
    peak_part[...] = jnp.full_like(peak_part, -jnp.inf)
    sum_part[...] = jnp.zeros_like(sum_part)
    acc[...] = jnp.zeros_like(acc)

    def fold(part, op):
        out = part[:, :lanes]
        for at in range(lanes, chunk, lanes):
            out = op(out, part[:, at:at + lanes])
        return out

    def score(step, carry):
        base = pl.multiple_of(step * chunk, chunk)
        part = jnp.dot(
            query[...], cache[which, :, pl.ds(base, chunk)], preferred_element_type=jnp.float32
        )
        slot = base + lax.broadcasted_iota(jnp.int32, (1, chunk), 1)
        part = jnp.where(slot <= limit, part, -jnp.inf)
        scores[:, pl.ds(base, chunk)] = part
        peak_part[...] = jnp.maximum(peak_part[...], fold(part, jnp.maximum))
        return carry

    lax.fori_loop(0, ctx // chunk, score, 0)
    peak = jnp.max(peak_part[...], axis=1, keepdims=True) * coef

    def weigh(step, carry):
        base = pl.multiple_of(step * chunk, chunk)
        part = jnp.exp2(scores[:, pl.ds(base, chunk)] * coef - peak)
        sum_part[...] += fold(part, jnp.add)
        acc[...] += lax.dot_general(
            part.astype(jnp.bfloat16), cache[which, :kv, pl.ds(base, chunk)],
            (((1,), (1,)), ((), ())), preferred_element_type=jnp.float32,
        )
        return carry

    lax.fori_loop(0, ctx // chunk, weigh, 0)
    return acc[...] * (1.0 / jnp.sum(sum_part[...], axis=1, keepdims=True))


def kernel(
    n, drafts, heads_here, nope, rope, kv, vd, coef, chunk,
    length_ref, start_ref, latent_ref, cache_hbm, wq_hbm, wk_hbm, wv_hbm,
    out_ref,
    cache, wq, wk, wv, gather, own_f32, q_full, wide_f32, rope_f32, turned_f32, send_q, send_r, recv_q, recv_r,
    query, scores, peak_part, sum_part, acc, send_o, recv_o,
    cache_sem, wq_sem, wk_sem, wv_sem, own_sem, ga_sem, gb_sem, gc_sem, ha_sem, hb_sem, hc_sem,
    sq_sem, sr_sem, so_sem, rq_sem, rr_sem, ro_sem,
):
    me = lax.axis_index("wide")
    owned = cache.shape[0]
    group = drafts * heads_here
    head_dim = nope + rope
    cores, lines, plane = gather.shape[:3]
    spots = lines * plane
    core, spot = lax.rem(me, cores), me // cores
    line, place = spot // plane, lax.rem(spot, plane)
    other = cores - 1 - core
    step, spot_step = spread_step(n), spread_step(spots)

    def partner(t):
        return lax.rem(me + lax.rem(t * step, n), n)

    load_q = pltpu.make_async_copy(wq_hbm, wq, wq_sem)
    load_k = pltpu.make_async_copy(wk_hbm, wk, wk_sem)
    load_v = pltpu.make_async_copy(wv_hbm, wv, wv_sem)
    loads = [
        pltpu.make_async_copy(cache_hbm.at[which], cache.at[which], cache_sem.at[which])
        for which in range(owned)
    ]
    barrier = pltpu.get_barrier_semaphore()

    def greet(t, carry):
        pl.semaphore_signal(barrier, inc=1, device_id={"wide": partner(t)}, device_id_type=MESH)
        return carry

    lax.fori_loop(1, n, greet, 0)
    load_q.start()
    load_k.start()
    for load in loads:
        load.start()
    load_v.start()

    for which in range(owned):
        own_f32[which * drafts:(which + 1) * drafts, :] = latent_ref[which].astype(jnp.float32)
    mine = own_f32[...]
    depth = mine.shape[1] // 2
    stacked = jnp.concatenate([mine[:, :depth], mine[:, depth:]], axis=0)
    gather[core, line, place] = stacked.astype(jnp.bfloat16)
    cosine, sine = rotary_tables(start_ref, drafts, group, rope, owned)
    pl.semaphore_wait(barrier, n - 1)

    def to_line(t, carry):
        there = lax.rem(line + t, lines)
        mine = gather.at[core, line, place]
        pltpu.make_async_remote_copy(
            src_ref=mine, dst_ref=mine, send_sem=ga_sem, recv_sem=ha_sem,
            device_id={"wide": (there * plane + place) * cores + core}, device_id_type=MESH,
        ).start()
        return carry

    def to_plane(t, carry):
        there = lax.rem(place + t, plane)
        mine = gather.at[core, :, place]
        pltpu.make_async_remote_copy(
            src_ref=mine, dst_ref=mine, send_sem=gb_sem, recv_sem=hb_sem,
            device_id={"wide": (line * plane + there) * cores + core}, device_id_type=MESH,
        ).start()
        return carry

    def landed(ref, sem):
        pltpu.make_async_copy(ref, ref, sem).wait()

    lax.fori_loop(1, lines, to_line, 0)
    landed(gather.at[core, pl.ds(0, lines - 1), place], ha_sem)
    lax.fori_loop(1, plane, to_plane, 0)
    landed(gather.at[core, :, pl.ds(0, plane - 1)], hb_sem)
    across = pltpu.make_async_remote_copy(
        src_ref=gather.at[core], dst_ref=gather.at[core], send_sem=gc_sem, recv_sem=hc_sem,
        device_id={"wide": spot * cores + other}, device_id_type=MESH,
    )
    across.start()

    def queries(side):
        rows = q_full.shape[0]
        latents = gather[side].reshape(spots, 2 * owned * drafts, depth).astype(jnp.float32)
        low = latents[:, :owned * drafts].reshape(rows, depth).astype(jnp.bfloat16)
        high = latents[:, owned * drafts:].reshape(rows, depth).astype(jnp.bfloat16)
        columns = heads_here * head_dim
        block = 256 if columns % 256 == 0 else columns
        for at in range(0, columns, block):
            part = jnp.dot(low, wq[:depth, at:at + block], preferred_element_type=jnp.float32)
            part += jnp.dot(high, wq[depth:, at:at + block], preferred_element_type=jnp.float32)
            q_full[:, at:at + block] = part.astype(jnp.bfloat16).astype(jnp.float32)
        for head in range(heads_here):
            at = head * head_dim
            absorbed = jnp.dot(
                q_full[:, at:at + nope].astype(jnp.bfloat16), wk[head],
                preferred_element_type=jnp.float32,
            )
            for part in range(kv // 128):
                wide_f32[part, pl.ds(head, rows, stride=heads_here), :] = absorbed[:, part * 128:part * 128 + 128]
            tail = q_full[:, at + nope:at + head_dim]
            rope_f32[pl.ds(head, rows, stride=heads_here), :] = jnp.concatenate([tail] * owned, axis=-1)
        for part in range(kv // 128):
            packed = wide_f32[part, :rows * heads_here].astype(jnp.bfloat16).reshape(spots, owned, group, 128)
            for which in range(owned):
                send_q[side, which, :, :, part * 128:part * 128 + 128] = packed[:, which]
        turned = rope_f32[:, :rope].reshape(spots, owned, group, rope)
        send_r[side] = jnp.concatenate(
            [turned[:, which] for which in range(owned)], axis=-1
        ).astype(jnp.bfloat16)

    sides = (core, other)

    def blocks(ref, kind):
        return ref.at[pl.ds(0, spots - 1)] if kind == 0 else ref

    def ship(source, sink, send_sem, recv_sem, kind):
        side = sides[kind]

        def post(t, carry):
            there = lax.rem(spot + lax.rem(t * spot_step, spots), spots)
            pltpu.make_async_remote_copy(
                src_ref=source.at[there], dst_ref=sink.at[core, spot],
                send_sem=send_sem, recv_sem=recv_sem,
                device_id={"wide": there * cores + side}, device_id_type=MESH,
            ).start()
            return carry

        lax.fori_loop(1 - kind, spots, post, 0)

    def ship_queries(which, kind):
        side = sides[kind]
        if which == 0:
            ship(send_r.at[side], recv_r, sr_sem.at[kind], rr_sem.at[kind], kind)
        ship(
            send_q.at[side, which], recv_q.at[which],
            sq_sem.at[which, kind], rq_sem.at[which, kind], kind,
        )

    def settle(ref, sem, kind):
        landed(blocks(ref, kind), sem)

    pieces = [(which, kind) for which in range(owned) for kind in range(2)]
    load_q.wait()
    load_k.wait()
    queries(core)
    ship_queries(0, 0)
    across.wait_recv()
    queries(other)
    ship_queries(0, 1)
    keep = [
        pltpu.make_async_copy(send_q.at[core, which, spot], recv_q.at[which, core, spot], own_sem.at[which])
        for which in range(owned)
    ] + [pltpu.make_async_copy(send_r.at[core, spot], recv_r.at[core, spot], own_sem.at[owned])]
    for copy in keep:
        copy.start()
    for copy in keep:
        copy.wait()

    def turn_queries(kind):
        settle(recv_r.at[sides[kind]], rr_sem.at[kind], kind)
        turn = recv_r[sides[kind]].astype(jnp.float32)
        width = turn.shape[2]
        flat = turn.reshape(spots * group, width)
        lane = lax.broadcasted_iota(jnp.int32, (1, width), 1)
        half = rope // 2
        swapped = jnp.where(
            lax.rem(lane, rope) < half,
            pltpu.roll(flat, width - half, 1),
            pltpu.roll(flat, half, 1),
        ).reshape(spots, group, width)
        rotated = turn * cosine[None] + swapped * sine[None]
        turned_f32[kind] = rotated.reshape(spots * group, width)

    for number, (which, kind) in enumerate(pieces):
        side = sides[kind]
        if number + 2 < len(pieces):
            settle(send_q.at[side, which], sq_sem.at[which, kind], kind)
            ship_queries(*pieces[number + 2])
        if which == 0:
            turn_queries(kind)
        settle(recv_q.at[which, side], rq_sem.at[which, kind], kind)
        query[:, :kv] = recv_q[which, side].reshape(spots * group, kv)
        query[:, kv:] = turned_f32[kind, :, which * rope:(which + 1) * rope].astype(jnp.bfloat16)
        if kind == 0:
            loads[which].wait()
        latents = attend(
            which, length_ref[which], query, cache, scores, peak_part, sum_part, acc,
            drafts, group, kv, coef, chunk,
        )
        send_o[which, side] = latents.astype(jnp.bfloat16).reshape(spots, group, kv)
        ship(
            send_o.at[which, side], recv_o.at[which],
            so_sem.at[which, kind], ro_sem.at[which, kind], kind,
        )
        if kind == 0:
            own = pltpu.make_async_copy(
                send_o.at[which, core, spot], recv_o.at[which, core, spot], own_sem.at[0]
            )
            own.start()
            own.wait()

    load_v.wait()
    rows = spots * drafts
    for which, kind in pieces:
        side = sides[kind]
        settle(recv_o.at[which, side], ro_sem.at[which, kind], kind)
        for part in range(kv // 128):
            arrived = recv_o[which, side, :, :, part * 128:part * 128 + 128]
            wide_f32[part, :spots * group] = arrived.astype(jnp.float32).reshape(spots * group, 128)
        for head in range(heads_here):
            mine = jnp.concatenate(
                [wide_f32[part, pl.ds(head, rows, stride=heads_here), :] for part in range(kv // 128)], axis=-1
            ).astype(jnp.bfloat16)
            value = jnp.dot(mine, wv[head], preferred_element_type=jnp.float32)
            out_ref[:, side, which, :, head * vd:(head + 1) * vd] = value.reshape(
                spots, drafts, vd
            ).astype(jnp.bfloat16)

    landed(gather.at[core, pl.ds(0, lines - 1), place], ga_sem)
    landed(gather.at[core, :, pl.ds(0, plane - 1)], gb_sem)
    across.wait_send()
    for kind in range(2):
        settle(send_r.at[sides[kind]], sr_sem.at[kind], kind)
    for number, (which, kind) in enumerate(pieces):
        if number + 2 >= len(pieces):
            settle(send_q.at[sides[kind], which], sq_sem.at[which, kind], kind)
        settle(send_o.at[which, sides[kind]], so_sem.at[which, kind], kind)


def per_device(q_latent, draft_start, cache_len, latent_cache, w_q_up, w_k_absorb, value_up_weight):
    n = lax.axis_size("wide")
    heads_here, nope, kv = w_k_absorb.shape
    vd = value_up_weight.shape[2]
    head_dim = w_q_up.shape[1] // heads_here
    rope = head_dim - nope
    owned, ctx, width = latent_cache.shape[1:]
    drafts, ql = q_latent.shape[2:]
    group = drafts * heads_here
    rows = n * owned * drafts
    chunk = min(1024, ctx)
    coef = float(head_dim) ** -0.5 * math.log2(math.e)
    bf16, f32 = jnp.bfloat16, jnp.float32

    wq = lax.all_gather(w_q_up, "batch", axis=0, tiled=True)
    cores, plane = 2, 4
    spots, lines = n // cores, n // (cores * plane)

    vmem = pl.BlockSpec(memory_space=pltpu.VMEM)
    smem = pl.BlockSpec(memory_space=pltpu.SMEM)
    hbm = pl.BlockSpec(memory_space=pl.ANY)
    dma = pltpu.SemaphoreType.DMA
    out = pl.pallas_call(
        functools.partial(kernel, n, drafts, heads_here, nope, rope, kv, vd, coef, chunk),
        out_shape=jax.ShapeDtypeStruct((spots, cores, owned, drafts, heads_here * vd), bf16),
        in_specs=[smem, smem, vmem, hbm, hbm, hbm, hbm],
        out_specs=vmem,
        scratch_shapes=[
            pltpu.VMEM((owned, width, ctx), bf16),
            pltpu.VMEM(wq.shape, bf16),
            pltpu.VMEM(w_k_absorb.shape, bf16),
            pltpu.VMEM(value_up_weight.shape, bf16),
            pltpu.VMEM((cores, lines, plane, 2 * owned * drafts, ql // 2), bf16),
            pltpu.VMEM((owned * drafts, ql), f32),
            pltpu.VMEM((rows // cores, heads_here * head_dim), f32),
            pltpu.VMEM((kv // 128, rows * heads_here // cores, 128), f32),
            pltpu.VMEM((rows * heads_here // cores, owned * rope), f32),
            pltpu.VMEM((cores, spots * group, owned * rope), f32),
            pltpu.VMEM((cores, owned, spots, group, kv), bf16),
            pltpu.VMEM((cores, spots, group, owned * rope), bf16),
            pltpu.VMEM((owned, cores, spots, group, kv), bf16),
            pltpu.VMEM((cores, spots, group, owned * rope), bf16),
            pltpu.VMEM((spots * group, width), bf16),
            pltpu.VMEM((spots * group, ctx), f32),
            pltpu.VMEM((spots * group, min(128, chunk)), f32),
            pltpu.VMEM((spots * group, min(128, chunk)), f32),
            pltpu.VMEM((spots * group, kv), f32),
            pltpu.VMEM((owned, cores, spots, group, kv), bf16),
            pltpu.VMEM((owned, cores, spots, group, kv), bf16),
            dma((owned,)), dma, dma, dma, dma((owned + 1,)), dma, dma, dma, dma, dma, dma,
            dma((owned, cores)), dma((cores,)), dma((owned, cores)),
            dma((owned, cores)), dma((cores,)), dma((owned, cores)),
        ],
        compiler_params=pltpu.CompilerParams(
            collective_id=0, has_side_effects=True, vmem_limit_bytes=56 << 20
        ),
    )(cache_len[0], draft_start[0], q_latent[0], jnp.swapaxes(latent_cache[0], 1, 2), wq, w_k_absorb, value_up_weight)
    return out.reshape(1, n * owned, drafts, heads_here * vd)


def solution(mesh):
    in_specs = (
        P("batch", "wide", None, None),
        P("batch", "wide"),
        P("batch", "wide"),
        P("batch", "wide", None, None),
        P("batch", "wide"),
        P("wide", None, None),
        P("wide", None, None),
    )
    out_specs = P("batch", None, None, "wide")
    return jax.shard_map(
        per_device, mesh=mesh, in_specs=in_specs, out_specs=out_specs, check_vma=False
    )
```

```python
import functools
import math
import jax
import jax.numpy as jnp
import numpy as np
from jax import lax
from jax.experimental import pallas as pl
from jax.experimental.pallas import tpu as pltpu
from jax.sharding import PartitionSpec as P

MESH = pl.DeviceIdType.MESH


def spread_step(count):
    step = max(1, int(count * 0.41))
    while math.gcd(step, count) != 1:
        step += 1
    return step


def rotary_tables(start_ref, drafts, group, rope_width, owned):
    shape = (group, owned * rope_width)
    row = lax.broadcasted_iota(jnp.int32, shape, 0) // (group // drafts)
    lane = lax.broadcasted_iota(jnp.int32, shape, 1)
    half = rope_width // 2
    freqs = 10000.0 ** (-np.arange(half) * 2.0 / rope_width)
    freq = jnp.zeros(shape, jnp.float32)
    for at in range(half):
        freq = jnp.where(lax.rem(lane, half) == at, np.float32(freqs[at]), freq)
    start = jnp.full(shape, start_ref[0], jnp.int32)
    for which in range(1, owned):
        start = jnp.where(lane // rope_width == which, start_ref[which], start)
    angle = (start + row).astype(jnp.float32) * freq
    turns = jnp.floor(angle * (0.5 / math.pi) + 0.5)
    angle = angle - turns * 6.28125
    angle = angle - turns * 0.0019340515136718750
    angle = angle - turns * 1.2556659146475769e-06
    sine = jnp.sin(angle)
    sine = jnp.where(lax.rem(lane, rope_width) < rope_width // 2, -sine, sine)
    return jnp.cos(angle), sine


def attend(which, length, query, cache, scores, peak_part, sum_part, acc, drafts, group, kv, coef, chunk):
    rows = query.shape[0]
    ctx = cache.shape[2]
    lanes = peak_part.shape[1]
    row = lax.broadcasted_iota(jnp.int32, (rows, 1), 0)
    limit = length + lax.rem(row, group) // (group // drafts)
    peak_part[...] = jnp.full_like(peak_part, -jnp.inf)
    sum_part[...] = jnp.zeros_like(sum_part)
    acc[...] = jnp.zeros_like(acc)

    def fold(part, op):
        out = part[:, :lanes]
        for at in range(lanes, chunk, lanes):
            out = op(out, part[:, at:at + lanes])
        return out

    def score(step, carry):
        base = pl.multiple_of(step * chunk, chunk)
        part = jnp.dot(
            query[...], cache[which, :, pl.ds(base, chunk)], preferred_element_type=jnp.float32
        )
        slot = base + lax.broadcasted_iota(jnp.int32, (1, chunk), 1)
        part = jnp.where(slot <= limit, part, -jnp.inf)
        scores[:, pl.ds(base, chunk)] = part
        peak_part[...] = jnp.maximum(peak_part[...], fold(part, jnp.maximum))
        return carry

    lax.fori_loop(0, ctx // chunk, score, 0)
    peak = jnp.max(peak_part[...], axis=1, keepdims=True) * coef

    def weigh(step, carry):
        base = pl.multiple_of(step * chunk, chunk)
        part = jnp.exp2(scores[:, pl.ds(base, chunk)] * coef - peak)
        sum_part[...] += fold(part, jnp.add)
        acc[...] += lax.dot_general(
            part.astype(jnp.bfloat16), cache[which, :kv, pl.ds(base, chunk)],
            (((1,), (1,)), ((), ())), preferred_element_type=jnp.float32,
        )
        return carry

    lax.fori_loop(0, ctx // chunk, weigh, 0)
    return acc[...] * (1.0 / jnp.sum(sum_part[...], axis=1, keepdims=True))


def kernel(
    n, drafts, heads_here, nope, rope, kv, vd, coef, chunk,
    length_ref, start_ref, latent_ref, cache_hbm, wq_hbm, wk_hbm, wv_hbm,
    out_ref,
    cache, wq, wk, wv, gather, own_f32, q_full, wide_f32, rope_f32, turned_f32, send_first, send_q, recv_first, recv_q,
    query, scores, peak_part, sum_part, acc, send_o, recv_o,
    cache_sem, wq_sem, wk_sem, wv_sem, own_sem, ga_sem, gb_sem, gc_sem, ha_sem, hb_sem, hc_sem,
    sq_sem, so_sem, rq_sem, ro_sem,
):
    me = lax.axis_index("wide")
    owned = cache.shape[0]
    group = drafts * heads_here
    head_dim = nope + rope
    cores, lines, plane = gather.shape[:3]
    spots = lines * plane
    core, spot = lax.rem(me, cores), me // cores
    line, place = spot // plane, lax.rem(spot, plane)
    other = cores - 1 - core
    step, spot_step = spread_step(n), spread_step(spots)

    def partner(t):
        return lax.rem(me + lax.rem(t * step, n), n)

    load_q = pltpu.make_async_copy(wq_hbm, wq, wq_sem)
    load_k = pltpu.make_async_copy(wk_hbm, wk, wk_sem)
    load_v = pltpu.make_async_copy(wv_hbm, wv, wv_sem)
    loads = [
        pltpu.make_async_copy(cache_hbm.at[which], cache.at[which], cache_sem.at[which])
        for which in range(owned)
    ]
    barrier = pltpu.get_barrier_semaphore()

    def greet(t, carry):
        pl.semaphore_signal(barrier, inc=1, device_id={"wide": partner(t)}, device_id_type=MESH)
        return carry

    lax.fori_loop(1, n, greet, 0)
    load_q.start()
    load_k.start()
    for load in loads:
        load.start()
    load_v.start()

    for which in range(owned):
        own_f32[which * drafts:(which + 1) * drafts, :] = latent_ref[which].astype(jnp.float32)
    mine = own_f32[...]
    depth = mine.shape[1] // 2
    stacked = jnp.concatenate([mine[:, :depth], mine[:, depth:]], axis=0)
    gather[core, line, place] = stacked.astype(jnp.bfloat16)
    cosine, sine = rotary_tables(start_ref, drafts, group, rope, owned)
    pl.semaphore_wait(barrier, n - 1)

    def to_line(t):
        there = lax.rem(line + t, lines)
        mine = gather.at[core, line, place]
        pltpu.make_async_remote_copy(
            src_ref=mine, dst_ref=mine, send_sem=ga_sem, recv_sem=ha_sem.at[t],
            device_id={"wide": (there * plane + place) * cores + core}, device_id_type=MESH,
        ).start()

    def to_plane(source):
        block = gather.at[core, source, place]
        for t in range(1, plane):
            there = lax.rem(place + t, plane)
            pltpu.make_async_remote_copy(
                src_ref=block, dst_ref=block, send_sem=gb_sem, recv_sem=hb_sem,
                device_id={"wide": (line * plane + there) * cores + core}, device_id_type=MESH,
            ).start()

    def landed(ref, sem):
        pltpu.make_async_copy(ref, ref, sem).wait()

    nearest = sorted(range(1, lines), key=lambda t: min(t, lines - t))
    for t in nearest[::-1]:
        to_line(t)
    to_plane(line)
    for t in nearest:
        source = lax.rem(line + lines - t, lines)
        landed(gather.at[core, source, place], ha_sem.at[t])
        to_plane(source)
    landed(gather.at[core, :, pl.ds(0, plane - 1)], hb_sem)
    across = pltpu.make_async_remote_copy(
        src_ref=gather.at[core], dst_ref=gather.at[core], send_sem=gc_sem, recv_sem=hc_sem,
        device_id={"wide": spot * cores + other}, device_id_type=MESH,
    )
    across.start()

    sends = [send_first] + [send_q.at[which] for which in range(owned - 1)]
    recvs = [recv_first] + [recv_q.at[which] for which in range(owned - 1)]

    def queries(side):
        rows = q_full.shape[0]
        latents = gather[side].reshape(spots, 2 * owned * drafts, depth).astype(jnp.float32)
        low = latents[:, :owned * drafts].reshape(rows, depth).astype(jnp.bfloat16)
        high = latents[:, owned * drafts:].reshape(rows, depth).astype(jnp.bfloat16)
        columns = heads_here * head_dim
        block = 256 if columns % 256 == 0 else columns
        for at in range(0, columns, block):
            part = jnp.dot(low, wq[:depth, at:at + block], preferred_element_type=jnp.float32)
            part += jnp.dot(high, wq[depth:, at:at + block], preferred_element_type=jnp.float32)
            q_full[:, at:at + block] = part.astype(jnp.bfloat16).astype(jnp.float32)
        for head in range(heads_here):
            at = head * head_dim
            absorbed = jnp.dot(
                q_full[:, at:at + nope].astype(jnp.bfloat16), wk[head],
                preferred_element_type=jnp.float32,
            )
            for part in range(kv // 128):
                wide_f32[part, pl.ds(head, rows, stride=heads_here), :] = absorbed[:, part * 128:part * 128 + 128]
            tail = q_full[:, at + nope:at + head_dim]
            rope_f32[pl.ds(head, rows, stride=heads_here), :] = jnp.concatenate([tail] * owned, axis=-1)
        for part in range(kv // 128):
            packed = wide_f32[part, :rows * heads_here].astype(jnp.bfloat16).reshape(spots, owned, group, 128)
            for which in range(owned):
                sends[which][side, :, :, part * 128:part * 128 + 128] = packed[:, which]
        turned = rope_f32[:, :rope].reshape(spots, owned, group, rope)
        send_first[side, :, :, kv:] = jnp.concatenate(
            [turned[:, which] for which in range(owned)], axis=-1
        ).astype(jnp.bfloat16)

    sides = (core, other)

    def blocks(ref, kind):
        return ref.at[pl.ds(0, spots - 1)] if kind == 0 else ref

    def ship(source, sink, send_sem, recv_sem, kind):
        side = sides[kind]

        def post(t, carry):
            there = lax.rem(spot + lax.rem(t * spot_step, spots), spots)
            pltpu.make_async_remote_copy(
                src_ref=source.at[there], dst_ref=sink.at[core, spot],
                send_sem=send_sem, recv_sem=recv_sem,
                device_id={"wide": there * cores + side}, device_id_type=MESH,
            ).start()
            return carry

        lax.fori_loop(1 - kind, spots, post, 0)

    def ship_queries(which, kind):
        ship(
            sends[which].at[sides[kind]], recvs[which],
            sq_sem.at[which, kind], rq_sem.at[which, kind], kind,
        )

    def settle(ref, sem, kind):
        landed(blocks(ref, kind), sem)

    pieces = [(which, kind) for which in range(owned) for kind in range(2)]
    load_q.wait()
    load_k.wait()
    queries(core)
    ship_queries(0, 0)
    across.wait_recv()
    queries(other)
    ship_queries(0, 1)
    for which in range(1, owned):
        for kind in range(2):
            ship_queries(which, kind)
    keep = [
        pltpu.make_async_copy(sends[which].at[core, spot], recvs[which].at[core, spot], own_sem.at[which])
        for which in range(owned)
    ]
    for copy in keep:
        copy.start()
    for copy in keep:
        copy.wait()

    def turn_queries(kind):
        turn = recv_first[sides[kind], :, :, kv:].astype(jnp.float32)
        width = turn.shape[2]
        flat = turn.reshape(spots * group, width)
        lane = lax.broadcasted_iota(jnp.int32, (1, width), 1)
        half = rope // 2
        swapped = jnp.where(
            lax.rem(lane, rope) < half,
            pltpu.roll(flat, width - half, 1),
            pltpu.roll(flat, half, 1),
        ).reshape(spots, group, width)
        rotated = turn * cosine[None] + swapped * sine[None]
        turned_f32[kind] = rotated.reshape(spots * group, width)

    for which, kind in pieces:
        side = sides[kind]
        settle(recvs[which].at[side], rq_sem.at[which, kind], kind)
        if which == 0:
            turn_queries(kind)
        query[:, :kv] = recvs[which][side, :, :, :kv].reshape(spots * group, kv)
        query[:, kv:] = turned_f32[kind, :, which * rope:(which + 1) * rope].astype(jnp.bfloat16)
        if kind == 0:
            loads[which].wait()
        latents = attend(
            which, length_ref[which], query, cache, scores, peak_part, sum_part, acc,
            drafts, group, kv, coef, chunk,
        )
        send_o[which, side] = latents.astype(jnp.bfloat16).reshape(spots, group, kv)
        ship(
            send_o.at[which, side], recv_o.at[which],
            so_sem.at[which, kind], ro_sem.at[which, kind], kind,
        )
        if kind == 0:
            own = pltpu.make_async_copy(
                send_o.at[which, core, spot], recv_o.at[which, core, spot], own_sem.at[0]
            )
            own.start()
            own.wait()

    load_v.wait()
    rows = spots * drafts
    for which, kind in pieces:
        side = sides[kind]
        settle(recv_o.at[which, side], ro_sem.at[which, kind], kind)
        for part in range(kv // 128):
            arrived = recv_o[which, side, :, :, part * 128:part * 128 + 128]
            wide_f32[part, :spots * group] = arrived.astype(jnp.float32).reshape(spots * group, 128)
        for head in range(heads_here):
            mine = jnp.concatenate(
                [wide_f32[part, pl.ds(head, rows, stride=heads_here), :] for part in range(kv // 128)], axis=-1
            ).astype(jnp.bfloat16)
            value = jnp.dot(mine, wv[head], preferred_element_type=jnp.float32)
            out_ref[:, side, which, :, head * vd:(head + 1) * vd] = value.reshape(
                spots, drafts, vd
            ).astype(jnp.bfloat16)

    landed(gather.at[core, pl.ds(0, lines - 1), place], ga_sem)
    landed(gather.at[core, :, pl.ds(0, plane - 1)], gb_sem)
    across.wait_send()
    for which, kind in pieces:
        settle(sends[which].at[sides[kind]], sq_sem.at[which, kind], kind)
        settle(send_o.at[which, sides[kind]], so_sem.at[which, kind], kind)


def per_device(q_latent, draft_start, cache_len, latent_cache, w_q_up, w_k_absorb, value_up_weight):
    n = lax.axis_size("wide")
    heads_here, nope, kv = w_k_absorb.shape
    vd = value_up_weight.shape[2]
    head_dim = w_q_up.shape[1] // heads_here
    rope = head_dim - nope
    owned, ctx, width = latent_cache.shape[1:]
    drafts, ql = q_latent.shape[2:]
    group = drafts * heads_here
    rows = n * owned * drafts
    chunk = min(1024, ctx)
    coef = float(head_dim) ** -0.5 * math.log2(math.e)
    bf16, f32 = jnp.bfloat16, jnp.float32

    wq = lax.all_gather(w_q_up, "batch", axis=0, tiled=True)
    cores, plane = 2, 4
    spots, lines = n // cores, n // (cores * plane)

    vmem = pl.BlockSpec(memory_space=pltpu.VMEM)
    smem = pl.BlockSpec(memory_space=pltpu.SMEM)
    hbm = pl.BlockSpec(memory_space=pl.ANY)
    dma = pltpu.SemaphoreType.DMA
    out = pl.pallas_call(
        functools.partial(kernel, n, drafts, heads_here, nope, rope, kv, vd, coef, chunk),
        out_shape=jax.ShapeDtypeStruct((spots, cores, owned, drafts, heads_here * vd), bf16),
        in_specs=[smem, smem, vmem, hbm, hbm, hbm, hbm],
        out_specs=vmem,
        scratch_shapes=[
            pltpu.VMEM((owned, width, ctx), bf16),
            pltpu.VMEM(wq.shape, bf16),
            pltpu.VMEM(w_k_absorb.shape, bf16),
            pltpu.VMEM(value_up_weight.shape, bf16),
            pltpu.VMEM((cores, lines, plane, 2 * owned * drafts, ql // 2), bf16),
            pltpu.VMEM((owned * drafts, ql), f32),
            pltpu.VMEM((rows // cores, heads_here * head_dim), f32),
            pltpu.VMEM((kv // 128, rows * heads_here // cores, 128), f32),
            pltpu.VMEM((rows * heads_here // cores, owned * rope), f32),
            pltpu.VMEM((cores, spots * group, owned * rope), f32),
            pltpu.VMEM((cores, spots, group, kv + owned * rope), bf16),
            pltpu.VMEM((max(owned - 1, 1), cores, spots, group, kv), bf16),
            pltpu.VMEM((cores, spots, group, kv + owned * rope), bf16),
            pltpu.VMEM((max(owned - 1, 1), cores, spots, group, kv), bf16),
            pltpu.VMEM((spots * group, width), bf16),
            pltpu.VMEM((spots * group, ctx), f32),
            pltpu.VMEM((spots * group, min(128, chunk)), f32),
            pltpu.VMEM((spots * group, min(128, chunk)), f32),
            pltpu.VMEM((spots * group, kv), f32),
            pltpu.VMEM((owned, cores, spots, group, kv), bf16),
            pltpu.VMEM((owned, cores, spots, group, kv), bf16),
            dma((owned,)), dma, dma, dma, dma((owned + 1,)), dma, dma, dma, dma((lines,)), dma, dma,
            dma((owned, cores)), dma((owned, cores)), dma((owned, cores)), dma((owned, cores)),
        ],
        compiler_params=pltpu.CompilerParams(
            collective_id=0, has_side_effects=True, vmem_limit_bytes=56 << 20
        ),
    )(cache_len[0], draft_start[0], q_latent[0], jnp.swapaxes(latent_cache[0], 1, 2), wq, w_k_absorb, value_up_weight)
    return out.reshape(1, n * owned, drafts, heads_here * vd)


def solution(mesh):
    in_specs = (
        P("batch", "wide", None, None),
        P("batch", "wide"),
        P("batch", "wide"),
        P("batch", "wide", None, None),
        P("batch", "wide"),
        P("wide", None, None),
        P("wide", None, None),
    )
    out_specs = P("batch", None, None, "wide")
    return jax.shard_map(
        per_device, mesh=mesh, in_specs=in_specs, out_specs=out_specs, check_vma=False
    )
```

```python
import functools
import math
import jax
import jax.numpy as jnp
import numpy as np
from jax import lax
from jax.experimental import pallas as pl
from jax.experimental.pallas import tpu as pltpu
from jax.sharding import PartitionSpec as P

MESH = pl.DeviceIdType.MESH


def spread_step(count):
    step = max(1, int(count * 0.41))
    while math.gcd(step, count) != 1:
        step += 1
    return step


def rotary_tables(start_ref, drafts, group, rope_width, owned):
    shape = (group, owned * rope_width)
    row = lax.broadcasted_iota(jnp.int32, shape, 0) // (group // drafts)
    lane = lax.broadcasted_iota(jnp.int32, shape, 1)
    half = rope_width // 2
    freqs = 10000.0 ** (-np.arange(half) * 2.0 / rope_width)
    freq = jnp.zeros(shape, jnp.float32)
    for at in range(half):
        freq = jnp.where(lax.rem(lane, half) == at, np.float32(freqs[at]), freq)
    start = jnp.full(shape, start_ref[0], jnp.int32)
    for which in range(1, owned):
        start = jnp.where(lane // rope_width == which, start_ref[which], start)
    angle = (start + row).astype(jnp.float32) * freq
    turns = jnp.floor(angle * (0.5 / math.pi) + 0.5)
    angle = angle - turns * 6.28125
    angle = angle - turns * 0.0019340515136718750
    angle = angle - turns * 1.2556659146475769e-06
    sine = jnp.sin(angle)
    sine = jnp.where(lax.rem(lane, rope_width) < rope_width // 2, -sine, sine)
    return jnp.cos(angle), sine


def attend(which, length, query, cache, flat, scores, peak_part, sum_part, acc, drafts, group, kv, coef, chunk):
    rows = query.shape[0]
    ctx = cache.shape[2]
    lanes = peak_part.shape[1]
    row = lax.broadcasted_iota(jnp.int32, (rows, 1), 0)
    limit = length + lax.rem(row, group) // (group // drafts)
    peak_part[...] = jnp.full_like(peak_part, -jnp.inf)
    sum_part[...] = jnp.zeros_like(sum_part)
    acc[...] = jnp.zeros_like(acc)

    def fold(part, op):
        out = part[:, :lanes]
        for at in range(lanes, chunk, lanes):
            out = op(out, part[:, at:at + lanes])
        return out

    def score(step, carry):
        base = pl.multiple_of(step * chunk, chunk)
        part = jnp.dot(
            query[...], cache[which, :, pl.ds(base, chunk)], preferred_element_type=jnp.float32
        )
        slot = base + lax.broadcasted_iota(jnp.int32, (1, chunk), 1)
        part = jnp.where(slot <= limit, part, -jnp.inf)
        scores[:, pl.ds(base, chunk)] = part
        peak_part[...] = jnp.maximum(peak_part[...], fold(part, jnp.maximum))
        return carry

    lax.fori_loop(0, ctx // chunk, score, 0)
    peak = jnp.max(peak_part[...], axis=1, keepdims=True) * coef

    def weigh(step, carry):
        base = pl.multiple_of(step * chunk, chunk)
        part = jnp.exp2(scores[:, pl.ds(base, chunk)] * coef - peak)
        sum_part[...] += fold(part, jnp.add)
        acc[...] += jnp.dot(
            part.astype(jnp.bfloat16), flat[which, pl.ds(base, chunk), :],
            preferred_element_type=jnp.float32,
        )
        return carry

    lax.fori_loop(0, ctx // chunk, weigh, 0)
    return acc[...] * (1.0 / jnp.sum(sum_part[...], axis=1, keepdims=True))


def kernel(
    n, drafts, heads_here, nope, rope, kv, vd, coef, chunk,
    length_ref, start_ref, latent_ref, cache_hbm, wq_hbm, wk_hbm, wv_hbm,
    out_ref,
    cache, flat, wq, wk, wv, gather, own_f32, q_full, wide_f32, rope_f32, turned_f32, send_first, send_q, recv_first, recv_q,
    query, scores, peak_part, sum_part, acc, send_o, recv_o,
    cache_sem, wq_sem, wk_sem, wv_sem, own_sem, ga_sem, gb_sem, gc_sem, ha_sem, hb_sem, hc_sem,
    sq_sem, so_sem, rq_sem, ro_sem,
):
    me = lax.axis_index("wide")
    owned = cache.shape[0]
    group = drafts * heads_here
    head_dim = nope + rope
    cores, lines, plane = gather.shape[:3]
    spots = lines * plane
    core, spot = lax.rem(me, cores), me // cores
    line, place = spot // plane, lax.rem(spot, plane)
    other = cores - 1 - core
    step, spot_step = spread_step(n), spread_step(spots)

    def partner(t):
        return lax.rem(me + lax.rem(t * step, n), n)

    load_q = pltpu.make_async_copy(wq_hbm, wq, wq_sem)
    load_k = pltpu.make_async_copy(wk_hbm, wk, wk_sem)
    load_v = pltpu.make_async_copy(wv_hbm, wv, wv_sem)
    loads = [
        pltpu.make_async_copy(cache_hbm.at[which], cache.at[which], cache_sem.at[which])
        for which in range(owned)
    ]
    barrier = pltpu.get_barrier_semaphore()

    def greet(t, carry):
        pl.semaphore_signal(barrier, inc=1, device_id={"wide": partner(t)}, device_id_type=MESH)
        return carry

    lax.fori_loop(1, n, greet, 0)
    load_q.start()
    load_k.start()
    for load in loads:
        load.start()
    load_v.start()

    for which in range(owned):
        own_f32[which * drafts:(which + 1) * drafts, :] = latent_ref[which].astype(jnp.float32)
    mine = own_f32[...]
    depth = mine.shape[1] // 2
    stacked = jnp.concatenate([mine[:, :depth], mine[:, depth:]], axis=0)
    gather[core, line, place] = stacked.astype(jnp.bfloat16)
    cosine, sine = rotary_tables(start_ref, drafts, group, rope, owned)
    pl.semaphore_wait(barrier, n - 1)

    def to_line(t):
        there = lax.rem(line + t, lines)
        mine = gather.at[core, line, place]
        pltpu.make_async_remote_copy(
            src_ref=mine, dst_ref=mine, send_sem=ga_sem, recv_sem=ha_sem.at[t],
            device_id={"wide": (there * plane + place) * cores + core}, device_id_type=MESH,
        ).start()

    def to_plane(source):
        block = gather.at[core, source, place]
        for t in range(1, plane):
            there = lax.rem(place + t, plane)
            pltpu.make_async_remote_copy(
                src_ref=block, dst_ref=block, send_sem=gb_sem, recv_sem=hb_sem,
                device_id={"wide": (line * plane + there) * cores + core}, device_id_type=MESH,
            ).start()

    def landed(ref, sem):
        pltpu.make_async_copy(ref, ref, sem).wait()

    nearest = sorted(range(1, lines), key=lambda t: min(t, lines - t))
    for t in nearest[::-1]:
        to_line(t)
    to_plane(line)
    for t in nearest:
        source = lax.rem(line + lines - t, lines)
        landed(gather.at[core, source, place], ha_sem.at[t])
        to_plane(source)
    def flatten(which):
        loads[which].wait()
        size = min(512, chunk)

        def turn(step, carry):
            base = pl.multiple_of(step * size, size)
            flat[which, pl.ds(base, size), :] = cache[which, :kv, pl.ds(base, size)].T
            return carry

        lax.fori_loop(0, cache.shape[2] // size, turn, 0)

    flatten(0)
    landed(gather.at[core, :, pl.ds(0, plane - 1)], hb_sem)
    across = pltpu.make_async_remote_copy(
        src_ref=gather.at[core], dst_ref=gather.at[core], send_sem=gc_sem, recv_sem=hc_sem,
        device_id={"wide": spot * cores + other}, device_id_type=MESH,
    )
    across.start()

    sends = [send_first] + [send_q.at[which] for which in range(owned - 1)]
    recvs = [recv_first] + [recv_q.at[which] for which in range(owned - 1)]

    def queries(side):
        rows = q_full.shape[0]
        latents = gather[side].reshape(spots, 2 * owned * drafts, depth).astype(jnp.float32)
        low = latents[:, :owned * drafts].reshape(rows, depth).astype(jnp.bfloat16)
        high = latents[:, owned * drafts:].reshape(rows, depth).astype(jnp.bfloat16)
        columns = heads_here * head_dim
        block = 256 if columns % 256 == 0 else columns
        for at in range(0, columns, block):
            part = jnp.dot(low, wq[:depth, at:at + block], preferred_element_type=jnp.float32)
            part += jnp.dot(high, wq[depth:, at:at + block], preferred_element_type=jnp.float32)
            q_full[:, at:at + block] = part.astype(jnp.bfloat16).astype(jnp.float32)
        for head in range(heads_here):
            at = head * head_dim
            absorbed = jnp.dot(
                q_full[:, at:at + nope].astype(jnp.bfloat16), wk[head],
                preferred_element_type=jnp.float32,
            )
            for part in range(kv // 128):
                wide_f32[part, pl.ds(head, rows, stride=heads_here), :] = absorbed[:, part * 128:part * 128 + 128]
            tail = q_full[:, at + nope:at + head_dim]
            rope_f32[pl.ds(head, rows, stride=heads_here), :] = jnp.concatenate([tail] * owned, axis=-1)
        for part in range(kv // 128):
            packed = wide_f32[part, :rows * heads_here].astype(jnp.bfloat16).reshape(spots, owned, group, 128)
            for which in range(owned):
                sends[which][side, :, :, part * 128:part * 128 + 128] = packed[:, which]
        turned = rope_f32[:, :rope].reshape(spots, owned, group, rope)
        send_first[side, :, :, kv:] = jnp.concatenate(
            [turned[:, which] for which in range(owned)], axis=-1
        ).astype(jnp.bfloat16)

    sides = (core, other)

    def blocks(ref, kind):
        return ref.at[pl.ds(0, spots - 1)] if kind == 0 else ref

    def ship(source, sink, send_sem, recv_sem, kind):
        side = sides[kind]

        def post(t, carry):
            there = lax.rem(spot + lax.rem(t * spot_step, spots), spots)
            pltpu.make_async_remote_copy(
                src_ref=source.at[there], dst_ref=sink.at[core, spot],
                send_sem=send_sem, recv_sem=recv_sem,
                device_id={"wide": there * cores + side}, device_id_type=MESH,
            ).start()
            return carry

        lax.fori_loop(1 - kind, spots, post, 0)

    def ship_queries(which, kind):
        ship(
            sends[which].at[sides[kind]], recvs[which],
            sq_sem.at[which, kind], rq_sem.at[which, kind], kind,
        )

    def settle(ref, sem, kind):
        landed(blocks(ref, kind), sem)

    pieces = [(which, kind) for which in range(owned) for kind in range(2)]
    load_q.wait()
    load_k.wait()
    queries(core)
    ship_queries(0, 0)
    across.wait_recv()
    queries(other)
    ship_queries(0, 1)
    for which in range(1, owned):
        for kind in range(2):
            ship_queries(which, kind)
    keep = [
        pltpu.make_async_copy(sends[which].at[core, spot], recvs[which].at[core, spot], own_sem.at[which])
        for which in range(owned)
    ]
    for copy in keep:
        copy.start()
    for copy in keep:
        copy.wait()

    for which in range(1, owned):
        flatten(which)

    def turn_queries(kind):
        turn = recv_first[sides[kind], :, :, kv:].astype(jnp.float32)
        width = turn.shape[2]
        flat = turn.reshape(spots * group, width)
        lane = lax.broadcasted_iota(jnp.int32, (1, width), 1)
        half = rope // 2
        swapped = jnp.where(
            lax.rem(lane, rope) < half,
            pltpu.roll(flat, width - half, 1),
            pltpu.roll(flat, half, 1),
        ).reshape(spots, group, width)
        rotated = turn * cosine[None] + swapped * sine[None]
        turned_f32[kind] = rotated.reshape(spots * group, width)

    for which, kind in pieces:
        side = sides[kind]
        settle(recvs[which].at[side], rq_sem.at[which, kind], kind)
        if which == 0:
            turn_queries(kind)
        query[:, :kv] = recvs[which][side, :, :, :kv].reshape(spots * group, kv)
        query[:, kv:] = turned_f32[kind, :, which * rope:(which + 1) * rope].astype(jnp.bfloat16)
        latents = attend(
            which, length_ref[which], query, cache, flat, scores, peak_part, sum_part, acc,
            drafts, group, kv, coef, chunk,
        )
        send_o[which, side] = latents.astype(jnp.bfloat16).reshape(spots, group, kv)
        ship(
            send_o.at[which, side], recv_o.at[which],
            so_sem.at[which, kind], ro_sem.at[which, kind], kind,
        )
        if kind == 0:
            own = pltpu.make_async_copy(
                send_o.at[which, core, spot], recv_o.at[which, core, spot], own_sem.at[0]
            )
            own.start()
            own.wait()

    load_v.wait()
    rows = spots * drafts
    for which, kind in pieces:
        side = sides[kind]
        settle(recv_o.at[which, side], ro_sem.at[which, kind], kind)
        for part in range(kv // 128):
            arrived = recv_o[which, side, :, :, part * 128:part * 128 + 128]
            wide_f32[part, :spots * group] = arrived.astype(jnp.float32).reshape(spots * group, 128)
        for head in range(heads_here):
            mine = jnp.concatenate(
                [wide_f32[part, pl.ds(head, rows, stride=heads_here), :] for part in range(kv // 128)], axis=-1
            ).astype(jnp.bfloat16)
            value = jnp.dot(mine, wv[head], preferred_element_type=jnp.float32)
            out_ref[:, side, which, :, head * vd:(head + 1) * vd] = value.reshape(
                spots, drafts, vd
            ).astype(jnp.bfloat16)

    landed(gather.at[core, pl.ds(0, lines - 1), place], ga_sem)
    landed(gather.at[core, :, pl.ds(0, plane - 1)], gb_sem)
    across.wait_send()
    for which, kind in pieces:
        settle(sends[which].at[sides[kind]], sq_sem.at[which, kind], kind)
        settle(send_o.at[which, sides[kind]], so_sem.at[which, kind], kind)


def per_device(q_latent, draft_start, cache_len, latent_cache, w_q_up, w_k_absorb, value_up_weight):
    n = lax.axis_size("wide")
    heads_here, nope, kv = w_k_absorb.shape
    vd = value_up_weight.shape[2]
    head_dim = w_q_up.shape[1] // heads_here
    rope = head_dim - nope
    owned, ctx, width = latent_cache.shape[1:]
    drafts, ql = q_latent.shape[2:]
    group = drafts * heads_here
    rows = n * owned * drafts
    chunk = min(1024, ctx)
    coef = float(head_dim) ** -0.5 * math.log2(math.e)
    bf16, f32 = jnp.bfloat16, jnp.float32

    wq = lax.all_gather(w_q_up, "batch", axis=0, tiled=True)
    cores, plane = 2, 4
    spots, lines = n // cores, n // (cores * plane)

    vmem = pl.BlockSpec(memory_space=pltpu.VMEM)
    smem = pl.BlockSpec(memory_space=pltpu.SMEM)
    hbm = pl.BlockSpec(memory_space=pl.ANY)
    dma = pltpu.SemaphoreType.DMA
    out = pl.pallas_call(
        functools.partial(kernel, n, drafts, heads_here, nope, rope, kv, vd, coef, chunk),
        out_shape=jax.ShapeDtypeStruct((spots, cores, owned, drafts, heads_here * vd), bf16),
        in_specs=[smem, smem, vmem, hbm, hbm, hbm, hbm],
        out_specs=vmem,
        scratch_shapes=[
            pltpu.VMEM((owned, width, ctx), bf16),
            pltpu.VMEM((owned, ctx, kv), bf16),
            pltpu.VMEM(wq.shape, bf16),
            pltpu.VMEM(w_k_absorb.shape, bf16),
            pltpu.VMEM(value_up_weight.shape, bf16),
            pltpu.VMEM((cores, lines, plane, 2 * owned * drafts, ql // 2), bf16),
            pltpu.VMEM((owned * drafts, ql), f32),
            pltpu.VMEM((rows // cores, heads_here * head_dim), f32),
            pltpu.VMEM((kv // 128, rows * heads_here // cores, 128), f32),
            pltpu.VMEM((rows * heads_here // cores, owned * rope), f32),
            pltpu.VMEM((cores, spots * group, owned * rope), f32),
            pltpu.VMEM((cores, spots, group, kv + owned * rope), bf16),
            pltpu.VMEM((max(owned - 1, 1), cores, spots, group, kv), bf16),
            pltpu.VMEM((cores, spots, group, kv + owned * rope), bf16),
            pltpu.VMEM((max(owned - 1, 1), cores, spots, group, kv), bf16),
            pltpu.VMEM((spots * group, width), bf16),
            pltpu.VMEM((spots * group, ctx), f32),
            pltpu.VMEM((spots * group, min(128, chunk)), f32),
            pltpu.VMEM((spots * group, min(128, chunk)), f32),
            pltpu.VMEM((spots * group, kv), f32),
            pltpu.VMEM((owned, cores, spots, group, kv), bf16),
            pltpu.VMEM((owned, cores, spots, group, kv), bf16),
            dma((owned,)), dma, dma, dma, dma((owned + 1,)), dma, dma, dma, dma((lines,)), dma, dma,
            dma((owned, cores)), dma((owned, cores)), dma((owned, cores)), dma((owned, cores)),
        ],
        compiler_params=pltpu.CompilerParams(
            collective_id=0, has_side_effects=True, vmem_limit_bytes=56 << 20
        ),
    )(cache_len[0], draft_start[0], q_latent[0], jnp.swapaxes(latent_cache[0], 1, 2), wq, w_k_absorb, value_up_weight)
    return out.reshape(1, n * owned, drafts, heads_here * vd)


def solution(mesh):
    in_specs = (
        P("batch", "wide", None, None),
        P("batch", "wide"),
        P("batch", "wide"),
        P("batch", "wide", None, None),
        P("batch", "wide"),
        P("wide", None, None),
        P("wide", None, None),
    )
    out_specs = P("batch", None, None, "wide")
    return jax.shard_map(
        per_device, mesh=mesh, in_specs=in_specs, out_specs=out_specs, check_vma=False
    )
```

```python
import functools
import math
import jax
import jax.numpy as jnp
import numpy as np
from jax import lax
from jax.experimental import pallas as pl
from jax.experimental.pallas import tpu as pltpu
from jax.sharding import PartitionSpec as P

MESH = pl.DeviceIdType.MESH


def spread_step(count):
    step = max(1, int(count * 0.41))
    while math.gcd(step, count) != 1:
        step += 1
    return step


def rotary_tables(start_ref, drafts, group, rope_width, owned):
    shape = (group, owned * rope_width)
    row = lax.broadcasted_iota(jnp.int32, shape, 0) // (group // drafts)
    lane = lax.broadcasted_iota(jnp.int32, shape, 1)
    half = rope_width // 2
    freqs = 10000.0 ** (-np.arange(half) * 2.0 / rope_width)
    freq = jnp.zeros(shape, jnp.float32)
    for at in range(half):
        freq = jnp.where(lax.rem(lane, half) == at, np.float32(freqs[at]), freq)
    start = jnp.full(shape, start_ref[0], jnp.int32)
    for which in range(1, owned):
        start = jnp.where(lane // rope_width == which, start_ref[which], start)
    angle = (start + row).astype(jnp.float32) * freq
    turns = jnp.floor(angle * (0.5 / math.pi) + 0.5)
    angle = angle - turns * 6.28125
    angle = angle - turns * 0.0019340515136718750
    angle = angle - turns * 1.2556659146475769e-06
    sine = jnp.sin(angle)
    sine = jnp.where(lax.rem(lane, rope_width) < rope_width // 2, -sine, sine)
    return jnp.cos(angle), sine


def attend(which, length, query, cache, flat, scores, peak_part, sum_part, acc, drafts, group, kv, coef, chunk):
    rows = query.shape[0]
    ctx = cache.shape[2]
    lanes = peak_part.shape[1]
    row = lax.broadcasted_iota(jnp.int32, (rows, 1), 0)
    limit = length + lax.rem(row, group) // (group // drafts)
    peak_part[...] = jnp.full_like(peak_part, -jnp.inf)
    sum_part[...] = jnp.zeros_like(sum_part)
    acc[...] = jnp.zeros_like(acc)

    def fold(part, op):
        out = part[:, :lanes]
        for at in range(lanes, chunk, lanes):
            out = op(out, part[:, at:at + lanes])
        return out

    def score(step, carry):
        base = pl.multiple_of(step * chunk, chunk)
        part = jnp.dot(
            query[...], cache[which, :, pl.ds(base, chunk)], preferred_element_type=jnp.float32
        )
        slot = base + lax.broadcasted_iota(jnp.int32, (1, chunk), 1)
        part = jnp.where(slot <= limit, part, -jnp.inf)
        scores[:, pl.ds(base, chunk)] = part
        peak_part[...] = jnp.maximum(peak_part[...], fold(part, jnp.maximum))
        return carry

    lax.fori_loop(0, ctx // chunk, score, 0, unroll=True)
    peak = jnp.max(peak_part[...], axis=1, keepdims=True) * coef

    def weigh(step, carry):
        base = pl.multiple_of(step * chunk, chunk)
        part = jnp.exp2(scores[:, pl.ds(base, chunk)] * coef - peak)
        sum_part[...] += fold(part, jnp.add)
        acc[...] += jnp.dot(
            part.astype(jnp.bfloat16), flat[which, pl.ds(base, chunk), :],
            preferred_element_type=jnp.float32,
        )
        return carry

    lax.fori_loop(0, ctx // chunk, weigh, 0, unroll=True)
    return acc[...] * (1.0 / jnp.sum(sum_part[...], axis=1, keepdims=True))


def kernel(
    n, drafts, heads_here, nope, rope, kv, vd, coef, chunk,
    length_ref, start_ref, latent_ref, cache_hbm, wq_hbm, wk_hbm, wv_hbm,
    out_ref,
    cache, flat, wq, wk, wv, gather, own_f32, q_full, wide_f32, rope_f32, turned_f32, send_first, send_q, recv_first, recv_q,
    query, scores, peak_part, sum_part, acc, send_o, recv_o,
    cache_sem, wq_sem, wk_sem, wv_sem, own_sem, ga_sem, gb_sem, gc_sem, ha_sem, hb_sem, hc_sem,
    sq_sem, so_sem, rq_sem, ro_sem,
):
    me = lax.axis_index("wide")
    owned = cache.shape[0]
    group = drafts * heads_here
    head_dim = nope + rope
    cores, lines, plane = gather.shape[:3]
    spots = lines * plane
    core, spot = lax.rem(me, cores), me // cores
    line, place = spot // plane, lax.rem(spot, plane)
    other = cores - 1 - core
    step, spot_step = spread_step(n), spread_step(spots)

    def partner(t):
        return lax.rem(me + lax.rem(t * step, n), n)

    load_q = pltpu.make_async_copy(wq_hbm, wq, wq_sem)
    load_k = pltpu.make_async_copy(wk_hbm, wk, wk_sem)
    load_v = pltpu.make_async_copy(wv_hbm, wv, wv_sem)
    loads = [
        pltpu.make_async_copy(cache_hbm.at[which], cache.at[which], cache_sem.at[which])
        for which in range(owned)
    ]
    barrier = pltpu.get_barrier_semaphore()

    def greet(t, carry):
        pl.semaphore_signal(barrier, inc=1, device_id={"wide": partner(t)}, device_id_type=MESH)
        return carry

    lax.fori_loop(1, n, greet, 0)
    load_q.start()
    load_k.start()
    for load in loads:
        load.start()
    load_v.start()

    for which in range(owned):
        own_f32[which * drafts:(which + 1) * drafts, :] = latent_ref[which].astype(jnp.float32)
    mine = own_f32[...]
    depth = mine.shape[1] // 2
    stacked = jnp.concatenate([mine[:, :depth], mine[:, depth:]], axis=0)
    gather[core, line, place] = stacked.astype(jnp.bfloat16)
    cosine, sine = rotary_tables(start_ref, drafts, group, rope, owned)
    pl.semaphore_wait(barrier, n - 1)

    def to_line(t):
        there = lax.rem(line + t, lines)
        mine = gather.at[core, line, place]
        pltpu.make_async_remote_copy(
            src_ref=mine, dst_ref=mine, send_sem=ga_sem, recv_sem=ha_sem.at[t],
            device_id={"wide": (there * plane + place) * cores + core}, device_id_type=MESH,
        ).start()

    def to_plane(source):
        block = gather.at[core, source, place]
        for t in range(1, plane):
            there = lax.rem(place + t, plane)
            pltpu.make_async_remote_copy(
                src_ref=block, dst_ref=block, send_sem=gb_sem, recv_sem=hb_sem,
                device_id={"wide": (line * plane + there) * cores + core}, device_id_type=MESH,
            ).start()

    def landed(ref, sem):
        pltpu.make_async_copy(ref, ref, sem).wait()

    nearest = sorted(range(1, lines), key=lambda t: min(t, lines - t))
    for t in nearest[::-1]:
        to_line(t)
    to_plane(line)
    for t in nearest:
        source = lax.rem(line + lines - t, lines)
        landed(gather.at[core, source, place], ha_sem.at[t])
        to_plane(source)
    def flatten(which):
        loads[which].wait()
        size = min(512, chunk)

        def turn(step, carry):
            base = pl.multiple_of(step * size, size)
            flat[which, pl.ds(base, size), :] = cache[which, :kv, pl.ds(base, size)].T
            return carry

        lax.fori_loop(0, cache.shape[2] // size, turn, 0)

    flatten(0)
    landed(gather.at[core, :, pl.ds(0, plane - 1)], hb_sem)
    across = pltpu.make_async_remote_copy(
        src_ref=gather.at[core], dst_ref=gather.at[core], send_sem=gc_sem, recv_sem=hc_sem,
        device_id={"wide": spot * cores + other}, device_id_type=MESH,
    )
    across.start()

    sends = [send_first] + [send_q.at[which] for which in range(owned - 1)]
    recvs = [recv_first] + [recv_q.at[which] for which in range(owned - 1)]

    def queries(side):
        rows = q_full.shape[0]
        latents = gather[side].reshape(spots, 2 * owned * drafts, depth).astype(jnp.float32)
        low = latents[:, :owned * drafts].reshape(rows, depth).astype(jnp.bfloat16)
        high = latents[:, owned * drafts:].reshape(rows, depth).astype(jnp.bfloat16)
        columns = heads_here * head_dim
        block = 256 if columns % 256 == 0 else columns
        for at in range(0, columns, block):
            part = jnp.dot(low, wq[:depth, at:at + block], preferred_element_type=jnp.float32)
            part += jnp.dot(high, wq[depth:, at:at + block], preferred_element_type=jnp.float32)
            q_full[:, at:at + block] = part.astype(jnp.bfloat16).astype(jnp.float32)
        for head in range(heads_here):
            at = head * head_dim
            absorbed = jnp.dot(
                q_full[:, at:at + nope].astype(jnp.bfloat16), wk[head],
                preferred_element_type=jnp.float32,
            )
            for part in range(kv // 128):
                wide_f32[part, pl.ds(head, rows, stride=heads_here), :] = absorbed[:, part * 128:part * 128 + 128]
            tail = q_full[:, at + nope:at + head_dim]
            rope_f32[pl.ds(head, rows, stride=heads_here), :] = jnp.concatenate([tail] * owned, axis=-1)
        for part in range(kv // 128):
            packed = wide_f32[part, :rows * heads_here].astype(jnp.bfloat16).reshape(spots, owned, group, 128)
            for which in range(owned):
                sends[which][side, :, :, part * 128:part * 128 + 128] = packed[:, which]
        turned = rope_f32[:, :rope].reshape(spots, owned, group, rope)
        send_first[side, :, :, kv:] = jnp.concatenate(
            [turned[:, which] for which in range(owned)], axis=-1
        ).astype(jnp.bfloat16)

    sides = (core, other)

    def blocks(ref, kind):
        return ref.at[pl.ds(0, spots - 1)] if kind == 0 else ref

    def ship(source, sink, send_sem, recv_sem, kind):
        side = sides[kind]

        def post(t, carry):
            there = lax.rem(spot + lax.rem(t * spot_step, spots), spots)
            pltpu.make_async_remote_copy(
                src_ref=source.at[there], dst_ref=sink.at[core, spot],
                send_sem=send_sem, recv_sem=recv_sem,
                device_id={"wide": there * cores + side}, device_id_type=MESH,
            ).start()
            return carry

        lax.fori_loop(1 - kind, spots, post, 0)

    def ship_queries(which, kind):
        ship(
            sends[which].at[sides[kind]], recvs[which],
            sq_sem.at[which, kind], rq_sem.at[which, kind], kind,
        )

    def settle(ref, sem, kind):
        landed(blocks(ref, kind), sem)

    pieces = [(which, kind) for which in range(owned) for kind in range(2)]
    load_q.wait()
    load_k.wait()
    queries(core)
    ship_queries(0, 0)
    across.wait_recv()
    queries(other)
    ship_queries(0, 1)
    for which in range(1, owned):
        for kind in range(2):
            ship_queries(which, kind)
    keep = [
        pltpu.make_async_copy(sends[which].at[core, spot], recvs[which].at[core, spot], own_sem.at[which])
        for which in range(owned)
    ]
    for copy in keep:
        copy.start()
    for copy in keep:
        copy.wait()

    for which in range(1, owned):
        flatten(which)

    def turn_queries(kind):
        turn = recv_first[sides[kind], :, :, kv:].astype(jnp.float32)
        width = turn.shape[2]
        flat = turn.reshape(spots * group, width)
        lane = lax.broadcasted_iota(jnp.int32, (1, width), 1)
        half = rope // 2
        swapped = jnp.where(
            lax.rem(lane, rope) < half,
            pltpu.roll(flat, width - half, 1),
            pltpu.roll(flat, half, 1),
        ).reshape(spots, group, width)
        rotated = turn * cosine[None] + swapped * sine[None]
        turned_f32[kind] = rotated.reshape(spots * group, width)

    for which, kind in pieces:
        side = sides[kind]
        settle(recvs[which].at[side], rq_sem.at[which, kind], kind)
        if which == 0:
            turn_queries(kind)
        query[:, :kv] = recvs[which][side, :, :, :kv].reshape(spots * group, kv)
        query[:, kv:] = turned_f32[kind, :, which * rope:(which + 1) * rope].astype(jnp.bfloat16)
        latents = attend(
            which, length_ref[which], query, cache, flat, scores, peak_part, sum_part, acc,
            drafts, group, kv, coef, chunk,
        )
        send_o[which, side] = latents.astype(jnp.bfloat16).reshape(spots, group, kv)
        ship(
            send_o.at[which, side], recv_o.at[which],
            so_sem.at[which, kind], ro_sem.at[which, kind], kind,
        )
        if kind == 0:
            own = pltpu.make_async_copy(
                send_o.at[which, core, spot], recv_o.at[which, core, spot], own_sem.at[0]
            )
            own.start()
            own.wait()

    load_v.wait()
    rows = spots * drafts
    for which, kind in pieces:
        side = sides[kind]
        settle(recv_o.at[which, side], ro_sem.at[which, kind], kind)
        for part in range(kv // 128):
            arrived = recv_o[which, side, :, :, part * 128:part * 128 + 128]
            wide_f32[part, :spots * group] = arrived.astype(jnp.float32).reshape(spots * group, 128)
        for head in range(heads_here):
            mine = jnp.concatenate(
                [wide_f32[part, pl.ds(head, rows, stride=heads_here), :] for part in range(kv // 128)], axis=-1
            ).astype(jnp.bfloat16)
            value = jnp.dot(mine, wv[head], preferred_element_type=jnp.float32)
            out_ref[:, side, which, :, head * vd:(head + 1) * vd] = value.reshape(
                spots, drafts, vd
            ).astype(jnp.bfloat16)

    landed(gather.at[core, pl.ds(0, lines - 1), place], ga_sem)
    landed(gather.at[core, :, pl.ds(0, plane - 1)], gb_sem)
    across.wait_send()
    for which, kind in pieces:
        settle(sends[which].at[sides[kind]], sq_sem.at[which, kind], kind)
        settle(send_o.at[which, sides[kind]], so_sem.at[which, kind], kind)


def per_device(q_latent, draft_start, cache_len, latent_cache, w_q_up, w_k_absorb, value_up_weight):
    n = lax.axis_size("wide")
    heads_here, nope, kv = w_k_absorb.shape
    vd = value_up_weight.shape[2]
    head_dim = w_q_up.shape[1] // heads_here
    rope = head_dim - nope
    owned, ctx, width = latent_cache.shape[1:]
    drafts, ql = q_latent.shape[2:]
    group = drafts * heads_here
    rows = n * owned * drafts
    chunk = min(1024, ctx)
    coef = float(head_dim) ** -0.5 * math.log2(math.e)
    bf16, f32 = jnp.bfloat16, jnp.float32

    wq = lax.all_gather(w_q_up, "batch", axis=0, tiled=True)
    cores, plane = 2, 4
    spots, lines = n // cores, n // (cores * plane)

    vmem = pl.BlockSpec(memory_space=pltpu.VMEM)
    smem = pl.BlockSpec(memory_space=pltpu.SMEM)
    hbm = pl.BlockSpec(memory_space=pl.ANY)
    dma = pltpu.SemaphoreType.DMA
    out = pl.pallas_call(
        functools.partial(kernel, n, drafts, heads_here, nope, rope, kv, vd, coef, chunk),
        out_shape=jax.ShapeDtypeStruct((spots, cores, owned, drafts, heads_here * vd), bf16),
        in_specs=[smem, smem, vmem, hbm, hbm, hbm, hbm],
        out_specs=vmem,
        scratch_shapes=[
            pltpu.VMEM((owned, width, ctx), bf16),
            pltpu.VMEM((owned, ctx, kv), bf16),
            pltpu.VMEM(wq.shape, bf16),
            pltpu.VMEM(w_k_absorb.shape, bf16),
            pltpu.VMEM(value_up_weight.shape, bf16),
            pltpu.VMEM((cores, lines, plane, 2 * owned * drafts, ql // 2), bf16),
            pltpu.VMEM((owned * drafts, ql), f32),
            pltpu.VMEM((rows // cores, heads_here * head_dim), f32),
            pltpu.VMEM((kv // 128, rows * heads_here // cores, 128), f32),
            pltpu.VMEM((rows * heads_here // cores, owned * rope), f32),
            pltpu.VMEM((cores, spots * group, owned * rope), f32),
            pltpu.VMEM((cores, spots, group, kv + owned * rope), bf16),
            pltpu.VMEM((max(owned - 1, 1), cores, spots, group, kv), bf16),
            pltpu.VMEM((cores, spots, group, kv + owned * rope), bf16),
            pltpu.VMEM((max(owned - 1, 1), cores, spots, group, kv), bf16),
            pltpu.VMEM((spots * group, width), bf16),
            pltpu.VMEM((spots * group, ctx), f32),
            pltpu.VMEM((spots * group, min(128, chunk)), f32),
            pltpu.VMEM((spots * group, min(128, chunk)), f32),
            pltpu.VMEM((spots * group, kv), f32),
            pltpu.VMEM((owned, cores, spots, group, kv), bf16),
            pltpu.VMEM((owned, cores, spots, group, kv), bf16),
            dma((owned,)), dma, dma, dma, dma((owned + 1,)), dma, dma, dma, dma((lines,)), dma, dma,
            dma((owned, cores)), dma((owned, cores)), dma((owned, cores)), dma((owned, cores)),
        ],
        compiler_params=pltpu.CompilerParams(
            collective_id=0, has_side_effects=True, vmem_limit_bytes=56 << 20
        ),
    )(cache_len[0], draft_start[0], q_latent[0], jnp.swapaxes(latent_cache[0], 1, 2), wq, w_k_absorb, value_up_weight)
    return out.reshape(1, n * owned, drafts, heads_here * vd)


def solution(mesh):
    in_specs = (
        P("batch", "wide", None, None),
        P("batch", "wide"),
        P("batch", "wide"),
        P("batch", "wide", None, None),
        P("batch", "wide"),
        P("wide", None, None),
        P("wide", None, None),
    )
    out_specs = P("batch", None, None, "wide")
    return jax.shard_map(
        per_device, mesh=mesh, in_specs=in_specs, out_specs=out_specs, check_vma=False
    )
```
